256 devices in a mesh: dom: 64 (over z, y, x_hi), chan: 4 (over x_lo, core).
Axes of the slice: x: 4 (x_hi: 2, x_lo: 2; x = x_hi * 2 + x_lo), y: 4, z: 8, core: 2. Of those that a mesh axis runs over, the one named last changes fastest.
Arguments:
- node_latent: bfloat16 [163840, 256], P('dom', 'chan'), may hold values from -6 to 6
- edge_latent: bfloat16 [1376256, 256], P(('dom', 'chan')), may hold values from -6 to 6
- senders: int32 [1376256], P(('dom', 'chan')), may hold values from 0 to 2559
- receivers: int32 [1376256], P(('dom', 'chan')), may hold values from 0 to 4607, as said below
- edge_count: int32 [64], P('dom'), may hold values from 7168 to 21504, as said below
- send_list: int32 [64, 64, 32], P('dom'), may hold values from 0 to 2559
- w_edge_in: bfloat16 [768, 256], replicated, may hold values from -0.21875 to 0.21875
- edge_in_bias: float32 [256], replicated, may hold values from -3 to 3
- w_edge_out: bfloat16 [256, 256], replicated, may hold values from -0.375 to 0.375
- edge_out_bias: float32 [256], replicated, may hold values from -3 to 3
- edge_gain: float32 [256], replicated, may hold values from 0.1 to 1.9
- edge_shift: float32 [256], replicated, may hold values from -3 to 3
- w_node_in: bfloat16 [512, 256], P(None, 'chan'), may hold values from -0.25 to 0.25
- node_in_bias: bfloat16 [256], P('chan'), may hold values from -3 to 3
- w_node_out: bfloat16 [256, 256], P('chan'), may hold values from -0.375 to 0.375
- node_out_bias: float32 [256], replicated, may hold values from -3 to 3
- node_gain: float32 [256], P('chan'), may hold values from 0.1 to 1.9
- node_shift: float32 [256], P('chan'), may hold values from -3 to 3
Outputs:
- node_new: bfloat16 [163840, 256], P('dom', 'chan')
- edge_new: bfloat16 [1376256, 256], P(('dom', 'chan'))
The draws below stay inside these ranges and needn't reach their ends.
Inputs may be any that keep to these rules, and one draw needn't show every extreme that they name: `senders`: edge blocks belong to the sender's partition. `receivers`: values from 2560 on name halo slots as in the reference program; about four in five edges name an own row. `edge_count`: some partition's block is full in every draw.
All inputs are finite; a program needn't handle non-finite values.
Results may differ from the reference program's by a relative error of at most 0.012.
Values may be sent and summed in bfloat16 or wider, within the bound.
A program may use at most 128 MiB of HBM per device.

```python
import jax
import jax.numpy as jnp
from jax import lax

D = 256
NODE_PART = 2560
SLOT = 32
PARTS_SIZE = 64
EDGE_PART = 21504
NODES = 163840
EDGES = 1376256


def draw_edge_count(key, part):
    key = jax.random.fold_in(key, 11)
    first_key, second_key = jax.random.split(key)
    capacity = EDGE_PART
    drawn = jax.random.randint(first_key, (PARTS_SIZE,), capacity // 3, capacity + 1)
    full_index = jax.random.randint(second_key, (), 0, PARTS_SIZE)
    return jnp.where(jnp.arange(PARTS_SIZE) == full_index, capacity, drawn).astype(jnp.int32)


def draw_receivers(key, part):
    key = jax.random.fold_in(key, 23)
    pick_key, own_key, halo_key = jax.random.split(key, 3)
    picks = jax.random.randint(pick_key, (EDGES,), 0, 5)
    own_rows = jax.random.randint(own_key, (EDGES,), 0, NODE_PART)
    halo_rows = jax.random.randint(halo_key, (EDGES,), NODE_PART, NODE_PART + PARTS_SIZE * SLOT)
    drawn = jnp.where(picks < 4, own_rows, halo_rows)
    position = jnp.arange(EDGES)
    drawn = jnp.where(position == 0, NODE_PART + PARTS_SIZE * SLOT - 1, drawn)
    drawn = jnp.where(position == 1, 0, drawn)
    return drawn.astype(jnp.int32)


def place_ends(result, key, smallest, largest):
    spot = [jax.random.randint(jax.random.fold_in(key, axis), (), 0, length) for axis, length in enumerate(result.shape)]
    widest = result.shape.index(max(result.shape))
    neighbour = spot[:widest] + [(spot[widest] + 1) % result.shape[widest]] + spot[widest + 1:]
    return result.at[tuple(spot)].set(smallest).at[tuple(neighbour)].set(largest)


def block_scale(stream_key, dims, shards, smallest, largest):
    level = 1.0
    for dim, parts in shards:
        heights = jax.random.uniform(jax.random.fold_in(jax.random.fold_in(stream_key, 6), dim), (parts,), jnp.float32, smallest / len(shards), largest / len(shards))
        level = level * jnp.repeat(jnp.exp(heights), dims[dim] // parts).reshape((-1,) + (1,) * (len(dims) - 1 - dim))
    return level


def scatter_about(stream_key, shape, deviation, bound, cuts=(), kind=jnp.bfloat16):
    array = jax.random.normal(stream_key, shape, jnp.float32) * deviation
    if len(cuts) > 0:
        array = block_scale(stream_key, shape, cuts, -0.22, 0.18) * array
    return jnp.clip(array, min=-bound, max=bound).astype(kind)


def setup_inputs(seed: int = 0) -> dict:
    arg_keys = jax.random.split(jax.random.key(seed), 19)
    return {
        "node_latent": scatter_about(arg_keys[0], (NODES, D), 1.0, 6.0, ((0, 64), (1, 4))),
        "edge_latent": scatter_about(arg_keys[1], (EDGES, D), 1.0, 6.0, ((0, 256),)),
        "senders": place_ends(jax.random.randint(arg_keys[2], (EDGES,), 0, NODE_PART), jax.random.fold_in(arg_keys[2], 1), 0, NODE_PART - 1).astype(jnp.int32),
        "receivers": draw_receivers(jax.random.fold_in(arg_keys[18], 71), 0),
        "edge_count": draw_edge_count(jax.random.fold_in(arg_keys[18], 71), 0),
        "send_list": place_ends(jax.random.randint(arg_keys[5], (PARTS_SIZE, PARTS_SIZE, SLOT), 0, NODE_PART), jax.random.fold_in(arg_keys[5], 1), 0, NODE_PART - 1).astype(jnp.int32),
        "w_edge_in": scatter_about(arg_keys[6], (3 * D, D), (3 * D) ** -0.5, 0.21875),
        "edge_in_bias": scatter_about(arg_keys[7], (D,), 0.5, 3.0, (), jnp.float32),
        "w_edge_out": scatter_about(arg_keys[8], (D, D), D ** -0.5, 0.375),
        "edge_out_bias": scatter_about(arg_keys[9], (D,), 0.5, 3.0, (), jnp.float32),
        "edge_gain": jnp.clip(1.0 + 0.18 * jax.random.normal(arg_keys[10], (D,), jnp.float32), 0.1, 1.9),
        "edge_shift": scatter_about(arg_keys[11], (D,), 0.5, 3.0, (), jnp.float32),
        "w_node_in": scatter_about(arg_keys[12], (2 * D, D), (2 * D) ** -0.5, 0.25, ((1, 4),)),
        "node_in_bias": scatter_about(arg_keys[13], (D,), 0.5, 3.0, ((0, 4),)),
        "w_node_out": scatter_about(arg_keys[14], (D, D), D ** -0.5, 0.375, ((0, 4),)),
        "node_out_bias": scatter_about(arg_keys[15], (D,), 0.5, 3.0, (), jnp.float32),
        "node_gain": jnp.clip(1.0 + 0.18 * jax.random.normal(arg_keys[16], (D,), jnp.float32), 0.1, 1.9),
        "node_shift": scatter_about(arg_keys[17], (D,), 0.5, 3.0, ((0, 4),), jnp.float32),
    }


def silu_rows(values):
    return values * jax.nn.sigmoid(values)

def normalize(values, scale_vec, shift_vec):
    row_mean = lax.optimization_barrier(jnp.mean(values, axis=-1, keepdims=True))
    centred = values - row_mean
    row_var = lax.optimization_barrier(jnp.mean(centred * centred, axis=-1, keepdims=True))
    return centred * lax.rsqrt(row_var + 1e-05) * scale_vec + shift_vec

def reference(node_latent, edge_latent, senders, receivers, edge_count, send_list, w_edge_in, edge_in_bias, w_edge_out, edge_out_bias, edge_gain, edge_shift, w_node_in, node_in_bias, w_node_out, node_out_bias, node_gain, node_shift):
    latent = D
    edge_blocks = edge_latent.reshape(PARTS_SIZE, EDGE_PART, latent)
    sender_blocks = senders.reshape(PARTS_SIZE, EDGE_PART)
    receiver_blocks = receivers.reshape(PARTS_SIZE, EDGE_PART)
    owners = jnp.arange(PARTS_SIZE, dtype=jnp.int32)

    def one_part(summed, inputs):
        part_index, edge_block, sender_block, receiver_block, live_count = inputs
        sender_rows = part_index * NODE_PART + sender_block
        halo_slot = jnp.maximum(receiver_block - NODE_PART, 0).astype(jnp.int32)
        source = (halo_slot // SLOT).astype(jnp.int32)
        remote = send_list[source, part_index, halo_slot % SLOT]
        receiver_rows = jnp.where(receiver_block < NODE_PART, part_index * NODE_PART + receiver_block, source * NODE_PART + remote).astype(jnp.int32)
        sender_feats = node_latent[sender_rows]
        receiver_feats = node_latent[receiver_rows]
        pre_edge = jnp.dot(edge_block, w_edge_in[:latent], preferred_element_type=jnp.float32)
        pre_edge = pre_edge + jnp.dot(sender_feats, w_edge_in[latent:2 * latent], preferred_element_type=jnp.float32)
        pre_edge = pre_edge + jnp.dot(receiver_feats, w_edge_in[2 * latent:], preferred_element_type=jnp.float32)
        edge_hidden = silu_rows(pre_edge + edge_in_bias).astype(jnp.bfloat16)
        edge_post = jnp.dot(edge_hidden, w_edge_out, preferred_element_type=jnp.float32) + edge_out_bias
        live_mask = (jnp.arange(EDGE_PART, dtype=jnp.int32) < live_count).astype(jnp.float32)[:, None]
        edge_new = (edge_block.astype(jnp.float32) + live_mask * normalize(edge_post, edge_gain, edge_shift)).astype(jnp.bfloat16)
        summed = summed.at[receiver_rows].add(edge_new.astype(jnp.float32) * live_mask)
        return (summed, edge_new)
    initial = jnp.zeros((NODES, latent), jnp.float32)
    summed, edge_new = lax.scan(one_part, initial, (owners, edge_blocks, sender_blocks, receiver_blocks, edge_count))
    summed_bf = summed.astype(jnp.bfloat16)
    node_pre = jnp.dot(node_latent, w_node_in[:latent], preferred_element_type=jnp.float32)
    node_pre = node_pre + jnp.dot(summed_bf, w_node_in[latent:], preferred_element_type=jnp.float32)
    node_hidden = silu_rows(node_pre + node_in_bias.astype(jnp.float32)).astype(jnp.bfloat16)
    node_post = jnp.dot(node_hidden, w_node_out, preferred_element_type=jnp.float32) + node_out_bias
    node_new = (node_latent.astype(jnp.float32) + normalize(node_post, node_gain, node_shift)).astype(jnp.bfloat16)
    return (node_new, edge_new.reshape(EDGES, latent))
```

```python
import functools

import jax
import jax.numpy as jnp
from jax import lax
from jax.experimental import pallas as pl
from jax.experimental.pallas import tpu as pltpu
from jax.sharding import PartitionSpec as P

LANES = 128
EDGE_TILE = 768
UNROLL = 16
COPIES = 4
CHUNK = 512


def silu_rows(values):
    return values * jax.nn.sigmoid(values)


def edge_kernel(
    senders, receivers, live, own_rows, edges, w_in, b_in, w_out, b_out, gain, shift,
    edge_new, sums, sent, received, gathered, messages, *partial,
):
    step = pl.program_id(0)
    tile, latent = edges.shape

    def project(weights, target, rows):
        def chunk(k, carry):
            start = pl.multiple_of(k * CHUNK, CHUNK)
            block = jnp.dot(
                own_rows[pl.ds(start, CHUNK), :], weights, preferred_element_type=jnp.float32
            )
            target[pl.ds(2 * start, CHUNK, stride=2), :] = block[:, :LANES]
            target[pl.ds(2 * start + 1, CHUNK, stride=2), :] = block[:, LANES:]
            return carry

        lax.fori_loop(0, rows // CHUNK, chunk, 0)

    @pl.when(step == 0)
    def _():
        project(w_in[latent : 2 * latent, :], sent, sent.shape[0] // 2)
        project(w_in[2 * latent :, :], received, received.shape[0] // 2)
        for part in partial:
            part[...] = jnp.zeros_like(part)

    base = step * tile

    def gather(k, carry):
        for u in range(UNROLL):
            j = k * UNROLL + u
            s = senders[base + j]
            r = receivers[base + j]
            gathered[pl.ds(2 * j, 2), :] = sent[pl.ds(2 * s, 2), :] + received[pl.ds(2 * r, 2), :]
        return carry

    lax.fori_loop(0, tile // UNROLL, gather, 0)

    latents = edges[...]
    pre = jnp.dot(latents, w_in[:latent, :], preferred_element_type=jnp.float32)
    low = pre[:, :LANES] + gathered[pl.ds(0, tile, stride=2), :]
    high = pre[:, LANES:] + gathered[pl.ds(1, tile, stride=2), :]
    hidden = silu_rows(jnp.concatenate([low, high], axis=1) + b_in[...]).astype(jnp.bfloat16)
    post = jnp.dot(hidden, w_out[...], preferred_element_type=jnp.float32) + b_out[...]
    centred = post - jnp.mean(post, axis=-1, keepdims=True)
    var = jnp.mean(centred * centred, axis=-1, keepdims=True)
    norm = centred * lax.rsqrt(var + 1e-05) * gain[...] + shift[...]
    row = lax.broadcasted_iota(jnp.int32, (tile, 1), 0) + base
    norm = jnp.where(row < live[0], norm, 0.0)
    new = (latents.astype(jnp.float32) + norm).astype(jnp.bfloat16)
    edge_new[...] = new
    wide = new.astype(jnp.float32)
    messages[pl.ds(0, tile, stride=2), :] = wide[:, :LANES]
    messages[pl.ds(1, tile, stride=2), :] = wide[:, LANES:]

    def add_row(j, part):
        rows = pl.ds(2 * receivers[base + j], 2)
        part[rows, :] = part[rows, :] + messages[pl.ds(2 * j, 2), :]

    def scatter(k, carry):
        for u in range(UNROLL):
            add_row(k * UNROLL + u, partial[u % COPIES])
        return carry

    def scatter_one(j, carry):
        add_row(j, partial[0])
        return carry

    count = jnp.clip(live[0] - base, 0, tile)
    whole = count // UNROLL
    lax.fori_loop(0, whole, scatter, 0)
    lax.fori_loop(whole * UNROLL, count, scatter_one, 0)

    @pl.when(step == pl.num_programs(0) - 1)
    def _():
        def chunk(k, carry):
            start = pl.multiple_of(k * CHUNK, CHUNK)
            low = partial[0][pl.ds(2 * start, CHUNK, stride=2), :]
            high = partial[0][pl.ds(2 * start + 1, CHUNK, stride=2), :]
            for part in partial[1:]:
                low += part[pl.ds(2 * start, CHUNK, stride=2), :]
                high += part[pl.ds(2 * start + 1, CHUNK, stride=2), :]
            sums[pl.ds(start, CHUNK), :] = jnp.concatenate([low, high], axis=1).astype(sums.dtype)
            return carry

        lax.fori_loop(0, sums.shape[0] // CHUNK, chunk, 0)


def edge_block(node_rows, senders, receivers, live, table, edges, w_in, b_in, w_out, b_out, gain, shift):
    edge_rows, latent = edges.shape
    table_rows = table.shape[0]
    tile = EDGE_TILE
    full = lambda array: pl.BlockSpec(array.shape, lambda i, *_: (0, 0))
    tiled = pl.BlockSpec((tile, latent), lambda i, *_: (i, 0))
    scratch = lambda rows: pltpu.VMEM((2 * rows, LANES), jnp.float32)
    b_in, b_out, gain, shift = (v.reshape(1, latent) for v in (b_in, b_out, gain, shift))
    return pl.pallas_call(
        edge_kernel,
        grid_spec=pltpu.PrefetchScalarGridSpec(
            num_scalar_prefetch=3,
            grid=(edge_rows // tile,),
            in_specs=[full(table), tiled, full(w_in), full(b_in), full(w_out)] + [full(b_in)] * 3,
            out_specs=[tiled, pl.BlockSpec((table_rows, latent), lambda i, *_: (0, 0))],
            scratch_shapes=[scratch(node_rows), scratch(table_rows), scratch(tile), scratch(tile)]
            + [scratch(table_rows)] * COPIES,
        ),
        out_shape=[
            jax.ShapeDtypeStruct((edge_rows, latent), jnp.bfloat16),
            jax.ShapeDtypeStruct((table_rows, latent), jnp.bfloat16),
        ],
        compiler_params=pltpu.CompilerParams(vmem_limit_bytes=54 * 2**20),
        name="edges",
    )(senders, receivers, live, table, edges, w_in, b_in, w_out, b_out, gain, shift)


def body(
    node_latent,
    edge_latent,
    senders,
    receivers,
    edge_count,
    send_list,
    w_edge_in,
    edge_in_bias,
    w_edge_out,
    edge_out_bias,
    edge_gain,
    edge_shift,
    w_node_in,
    node_in_bias,
    w_node_out,
    node_out_bias,
    node_gain,
    node_shift,
):
    node_rows, quarter = node_latent.shape
    latent = w_edge_out.shape[0]
    part_count = lax.axis_size("dom")
    chan_size = lax.axis_size("chan")
    send_rows = send_list[0]
    slot_count = send_rows.shape[1]
    chan_index = lax.axis_index("chan")
    node_weights = lax.all_gather(
        jnp.concatenate([w_node_in.T, w_node_out], axis=1), "chan", axis=0, tiled=True
    )
    node_vectors = lax.all_gather(
        jnp.stack([node_in_bias.astype(jnp.float32), node_gain, node_shift]), "chan", axis=1, tiled=True
    )
    outgoing = node_latent[send_rows.reshape(-1)].reshape(part_count, slot_count, quarter)
    incoming = lax.all_to_all(outgoing, "dom", split_axis=0, concat_axis=0, tiled=True)
    table = jnp.concatenate(
        [node_latent, incoming.reshape(part_count * slot_count, quarter)], axis=0
    )
    table = lax.all_gather(table, "chan", axis=1, tiled=True)
    edge_rows = edge_latent.shape[0]
    live = jnp.clip(edge_count - chan_index * edge_rows, 0, edge_rows)
    edge_new, sums = edge_block(
        node_rows, senders, receivers, live, table, edge_latent, w_edge_in, edge_in_bias, w_edge_out,
        edge_out_bias, edge_gain, edge_shift,
    )
    halo = lax.psum_scatter(
        sums[node_rows:].reshape(part_count, slot_count, latent), "chan", scatter_dimension=1, tiled=True
    )
    returned = lax.all_to_all(halo, "dom", split_axis=0, concat_axis=0, tiled=True)
    slots = slot_count // chan_size
    my_rows = lax.dynamic_slice_in_dim(send_rows, chan_index * slots, slots, 1)
    local = sums[:node_rows].astype(jnp.float32) + jax.ops.segment_sum(
        returned.astype(jnp.float32).reshape(-1, latent), my_rows.reshape(-1), num_segments=node_rows
    )
    own = node_rows // chan_size
    summed = lax.psum_scatter(local, "chan", scatter_dimension=0, tiled=True).astype(jnp.bfloat16)
    nodes = lax.dynamic_slice_in_dim(table, chan_index * own, own, 0)
    across = (((1,), (1,)), ((), ()))
    pre = lax.dot_general(
        nodes, node_weights[:, :latent], across, preferred_element_type=jnp.float32
    ) + lax.dot_general(
        summed, node_weights[:, latent : 2 * latent], across, preferred_element_type=jnp.float32
    )
    hidden = silu_rows(pre + node_vectors[0]).astype(jnp.bfloat16)
    post = (
        jnp.dot(hidden, node_weights[:, 2 * latent :], preferred_element_type=jnp.float32) + node_out_bias
    )
    centred = post - jnp.mean(post, axis=-1, keepdims=True)
    var = jnp.mean(centred * centred, axis=-1, keepdims=True)
    norm = centred * lax.rsqrt(var + 1e-05) * node_vectors[1] + node_vectors[2]
    new = (nodes.astype(jnp.float32) + norm).astype(jnp.bfloat16)
    node_new = lax.all_to_all(new, "chan", split_axis=1, concat_axis=0, tiled=True)
    return (node_new, edge_new)


def solution(mesh):
    placed = (
        P("dom", "chan"),
        P(("dom", "chan"), None),
        P(("dom", "chan")),
        P(("dom", "chan")),
        P("dom"),
        P("dom", None, None),
        P(),
        P(),
        P(),
        P(),
        P(),
        P(),
        P(None, "chan"),
        P("chan"),
        P("chan", None),
        P(),
        P("chan"),
        P("chan"),
    )
    return jax.shard_map(
        body,
        mesh=mesh,
        in_specs=placed,
        out_specs=(P("dom", "chan"), P(("dom", "chan"), None)),
        check_vma=False,
    )
```

```python
import functools

import jax
import jax.numpy as jnp
from jax import lax
from jax.experimental import pallas as pl
from jax.experimental.pallas import tpu as pltpu
from jax.sharding import PartitionSpec as P

LANES = 128
EDGE_TILE = 768
UNROLL = 16
COPIES = 4
CHUNK = 512
GROUPS = 4
MESH = pl.DeviceIdType.MESH
FLOAT = jnp.float32
HALF = jnp.bfloat16
ANY = pl.BlockSpec(memory_space=pl.ANY)
VMEM = pl.BlockSpec(memory_space=pltpu.VMEM)


def silu_rows(values):
    return values * jax.nn.sigmoid(values)


def enter(dom, chan, parts, chans):
    barrier = pltpu.get_barrier_semaphore()

    def greet(k, carry):
        pl.semaphore_signal(barrier, inc=1, device_id=(lax.rem(dom + k, parts), chan), device_id_type=MESH)
        return carry

    lax.fori_loop(1, parts, greet, 0)
    for k in range(1, chans):
        pl.semaphore_signal(barrier, inc=1, device_id=(dom, lax.rem(chan + k, chans)), device_id_type=MESH)
    pl.semaphore_wait(barrier, parts + chans - 2)


def forward_kernel(
    send_rows, nodes, w_in, w_out, vectors,
    own, halo, all_in, all_out, all_vectors,
    wide, stage, outgoing, part_send, part_recv, send, recv, local,
    *, parts, chans,
):
    dom = lax.axis_index("dom")
    chan = lax.axis_index("chan")
    quarter, node_rows = nodes.shape
    slots = send_rows.shape[0] // 2
    sibling = (dom, chan + 1 - 2 * lax.rem(chan, 2))
    across = (dom, lax.rem(chan + 2, chans))
    far = lax.rem(chan + 2, chans)
    enter(dom, chan, parts, chans)

    def block(array, index):
        rows = array.shape[0] // chans
        return array.at[pl.ds(pl.multiple_of(index * rows, rows), rows), :]

    def push(src, dst, index, target):
        copy = pltpu.make_async_remote_copy(
            src_ref=src, dst_ref=dst, send_sem=send.at[index], recv_sem=recv.at[index],
            device_id=target, device_id_type=MESH,
        )
        copy.start()
        return copy

    gathered = [(nodes, own), (w_in, all_in), (w_out, all_out), (vectors, all_vectors)]
    near, wait_later, kept = [], [], []
    for index, (src, dst) in enumerate(gathered):
        near.append(push(src, block(dst, chan), 3 * index, across))
        wait_later.append(push(src, block(dst, chan), 3 * index + 1, sibling))
        keep = pltpu.make_async_copy(src, block(dst, chan), local.at[index])
        keep.start()
        kept.append(keep)

    for start in range(0, node_rows, LANES):
        piece = nodes[:, start : start + LANES].astype(FLOAT)
        wide[pl.ds(start, LANES), :] = jnp.concatenate([piece, piece], axis=0).T

    lane = lax.broadcasted_iota(jnp.int32, (1, LANES), 1)
    left = lane < quarter

    def fill(k):
        peer = lax.rem(dom + k + 1, parts)
        base = pl.multiple_of(k * slots, slots)
        for j in range(slots):
            low = wide[pl.ds(send_rows[j, peer], 1), :]
            high = wide[pl.ds(send_rows[j + slots, peer], 1), :]
            stage[pl.ds(base + j, 1), :] = jnp.where(left, low, high)
        outgoing[k] = stage[pl.ds(base, slots), :].astype(HALF)
        return peer, base

    group = parts // GROUPS

    def send_part(k, carry):
        peer, base = fill(k)
        pltpu.make_async_remote_copy(
            src_ref=outgoing.at[k], dst_ref=halo.at[chan, pl.ds(base, slots), :],
            send_sem=part_send, recv_sem=part_recv.at[k // group],
            device_id=(peer, chan), device_id_type=MESH,
        ).start()
        return carry

    lax.fori_loop(0, parts - 1, send_part, 0)
    _, base = fill(parts - 1)
    mine = pltpu.make_async_copy(
        outgoing.at[parts - 1], halo.at[chan, pl.ds(base, slots), :], part_recv.at[GROUPS - 1]
    )
    mine.start()

    relays = []
    for index, (src, dst) in enumerate(gathered):
        near[index].wait_recv()
        relays.append(push(block(dst, far), block(dst, far), 3 * index + 2, sibling))

    first = 3 * len(gathered)
    pieces = []
    for g in range(GROUPS):
        rows = pl.ds(g * group * slots, group * slots)
        piece = halo.at[chan, rows, :]
        pltpu.make_async_copy(piece, piece, part_recv.at[g]).wait()
        cross = push(piece, piece, first + 3 * g, across)
        wait_later.append(push(piece, piece, first + 3 * g + 1, sibling))
        pieces.append((rows, cross))
    for g, (rows, cross) in enumerate(pieces):
        cross.wait_recv()
        piece = halo.at[far, rows, :]
        relays.append(push(piece, piece, first + 3 * g + 2, sibling))
    for copy in wait_later + relays:
        copy.wait()
    for copy in near + [cross for _, cross in pieces]:
        copy.wait_send()
    for copy in kept:
        copy.wait()
    sent = outgoing.at[pl.ds(0, parts - 1)]
    pltpu.make_async_copy(sent, sent, part_send).wait()


def forward(send_rows, nodes, w_in, w_out, vectors, parts, chans):
    quarter, node_rows = nodes.shape
    slots = send_rows.shape[0]
    rows = parts * slots // 2
    copies = 3 * (4 + GROUPS)
    like = lambda array: jax.ShapeDtypeStruct((chans * array.shape[0], array.shape[1]), array.dtype)
    return pl.pallas_call(
        functools.partial(forward_kernel, parts=parts, chans=chans),
        in_specs=[pl.BlockSpec(memory_space=pltpu.SMEM)] + [VMEM] * 4,
        out_specs=[ANY] * 5,
        out_shape=[
            like(nodes), jax.ShapeDtypeStruct((chans, rows, LANES), HALF), like(w_in), like(w_out), like(vectors)
        ],
        scratch_shapes=[
            pltpu.VMEM((node_rows, LANES), FLOAT),
            pltpu.VMEM((rows, LANES), FLOAT),
            pltpu.VMEM((parts, slots // 2, LANES), HALF),
            pltpu.SemaphoreType.DMA,
            pltpu.SemaphoreType.DMA((GROUPS,)),
            pltpu.SemaphoreType.DMA((copies,)),
            pltpu.SemaphoreType.DMA((copies,)),
            pltpu.SemaphoreType.DMA((4,)),
        ],
        compiler_params=pltpu.CompilerParams(
            collective_id=0, has_side_effects=True, vmem_limit_bytes=24 * 2**20
        ),
        name="forward",
    )(send_rows, nodes, w_in, w_out, vectors)


def edge_kernel(
    senders, receivers, live, own, halo, edges, w_in, b_in, w_out, b_out, gain, shift,
    edge_new, sums, sent, received, gathered, messages, *partial,
):
    step = pl.program_id(0)
    tile, latent = edges.shape
    node_rows = own.shape[1]
    chans, halo_rows, _ = halo.shape
    quarter = latent // chans
    slots = 16

    @pl.when(step == 0)
    def _():
        across = (((0,), (0,)), ((), ()))
        for start in range(0, node_rows, CHUNK):
            block = own[:, start : start + CHUNK]
            for target, first in ((sent, latent), (received, 2 * latent)):
                result = lax.dot_general(
                    block, w_in[first : first + latent, :], across, preferred_element_type=FLOAT
                )
                target[pl.ds(2 * start, CHUNK, stride=2), :] = result[:, :LANES]
                target[pl.ds(2 * start + 1, CHUNK, stride=2), :] = result[:, LANES:]
        weights = [w_in[2 * latent + c * quarter : 2 * latent + (c + 1) * quarter, :] for c in range(chans)]
        zero = jnp.zeros_like(weights[0])
        halves = []
        for side in range(2):
            padded = [[w, zero] if side == 0 else [zero, w] for w in weights]
            halves.append([
                jnp.concatenate(padded[c] + padded[c + 1], axis=0) for c in range(0, chans, 2)
            ])
        for start in range(0, halo_rows, CHUNK):
            blocks = [
                jnp.concatenate([halo[c, start : start + CHUNK, :], halo[c + 1, start : start + CHUNK, :]], axis=1)
                for c in range(0, chans, 2)
            ]
            for side in range(2):
                result = sum(
                    jnp.dot(b, w, preferred_element_type=FLOAT) for b, w in zip(blocks, halves[side])
                )
                for lanes in range(2):
                    part = result[:, lanes * LANES : (lanes + 1) * LANES].reshape(CHUNK // slots, 2, 8, LANES)
                    for g in range(2):
                        at = node_rows + (2 * side + g) * (halo_rows // 2) + start // 2
                        received[pl.ds(2 * at + lanes, CHUNK // 2, stride=2), :] = part[:, g].reshape(
                            CHUNK // 2, LANES
                        )
        for part in partial:
            part[...] = jnp.zeros_like(part)

    base = step * tile

    def gather(k, carry):
        for u in range(UNROLL):
            j = k * UNROLL + u
            s = senders[base + j]
            r = receivers[base + j]
            gathered[pl.ds(2 * j, 2), :] = sent[pl.ds(2 * s, 2), :] + received[pl.ds(2 * r, 2), :]
        return carry

    lax.fori_loop(0, tile // UNROLL, gather, 0)

    latents = edges[...]
    pre = jnp.dot(latents, w_in[:latent, :], preferred_element_type=FLOAT)
    low = pre[:, :LANES] + gathered[pl.ds(0, tile, stride=2), :]
    high = pre[:, LANES:] + gathered[pl.ds(1, tile, stride=2), :]
    hidden = silu_rows(jnp.concatenate([low, high], axis=1) + b_in[...]).astype(HALF)
    post = jnp.dot(hidden, w_out[...], preferred_element_type=FLOAT) + b_out[...]
    centred = post - jnp.mean(post, axis=-1, keepdims=True)
    var = jnp.mean(centred * centred, axis=-1, keepdims=True)
    norm = centred * lax.rsqrt(var + 1e-05) * gain[...] + shift[...]
    row = lax.broadcasted_iota(jnp.int32, (tile, 1), 0) + base
    norm = jnp.where(row < live[0], norm, 0.0)
    new = (latents.astype(FLOAT) + norm).astype(HALF)
    edge_new[...] = new
    full = new.astype(FLOAT)
    messages[pl.ds(0, tile, stride=2), :] = full[:, :LANES]
    messages[pl.ds(1, tile, stride=2), :] = full[:, LANES:]

    def add_row(j, part):
        rows = pl.ds(2 * receivers[base + j], 2)
        part[rows, :] = part[rows, :] + messages[pl.ds(2 * j, 2), :]

    def scatter(k, carry):
        for u in range(UNROLL):
            add_row(k * UNROLL + u, partial[u % COPIES])
        return carry

    def scatter_one(j, carry):
        add_row(j, partial[0])
        return carry

    count = jnp.clip(live[0] - base, 0, tile)
    whole = count // UNROLL
    lax.fori_loop(0, whole, scatter, 0)
    lax.fori_loop(whole * UNROLL, count, scatter_one, 0)

    @pl.when(step == pl.num_programs(0) - 1)
    def _():
        def chunk(k, carry):
            rows = pl.ds(pl.multiple_of(k * CHUNK, CHUNK), CHUNK)
            total = partial[0][rows, :]
            for part in partial[1:]:
                total += part[rows, :]
            sums[rows, :] = total.astype(sums.dtype)
            return carry

        lax.fori_loop(0, sums.shape[0] // CHUNK, chunk, 0)


def edge_block(senders, receivers, live, own, halo, edges, w_in, b_in, w_out, b_out, gain, shift):
    edge_rows, latent = edges.shape
    node_rows = own.shape[1]
    table_rows = node_rows + 2 * halo.shape[1]
    tile = EDGE_TILE
    full = lambda array: pl.BlockSpec(array.shape, lambda i, *_: (0,) * array.ndim)
    tiled = pl.BlockSpec((tile, latent), lambda i, *_: (i, 0))
    scratch = lambda rows: pltpu.VMEM((2 * rows, LANES), FLOAT)
    b_in, b_out, gain, shift = (v.reshape(1, latent) for v in (b_in, b_out, gain, shift))
    return pl.pallas_call(
        edge_kernel,
        grid_spec=pltpu.PrefetchScalarGridSpec(
            num_scalar_prefetch=3,
            grid=(edge_rows // tile,),
            in_specs=[full(own), full(halo), tiled, full(w_in), full(b_in), full(w_out)] + [full(b_in)] * 3,
            out_specs=[tiled, pl.BlockSpec((2 * table_rows, LANES), lambda i, *_: (0, 0))],
            scratch_shapes=[scratch(node_rows), scratch(table_rows), scratch(tile), scratch(tile)]
            + [scratch(table_rows)] * COPIES,
        ),
        out_shape=[
            jax.ShapeDtypeStruct((edge_rows, latent), HALF),
            jax.ShapeDtypeStruct((2 * table_rows, LANES), HALF),
        ],
        compiler_params=pltpu.CompilerParams(vmem_limit_bytes=54 * 2**20),
        name="edges",
    )(senders, receivers, live, own, halo, edges, w_in, b_in, w_out, b_out, gain, shift)


def reverse_kernel(
    sums, own, rows_of, w_in, w_out, vectors,
    result,
    halo_in, own_in, halo_out, own_out, halo_far, own_far, reduced, returned, spread, own_sum, pick, nodes, fresh,
    part_send, part_recv, send, recv, local,
    *, parts, chans,
):
    dom = lax.axis_index("dom")
    chan = lax.axis_index("chan")
    side = chan // 2
    core = lax.rem(chan, 2)
    other = 1 - side
    far = lax.rem(chan + 2, chans)
    sibling = (dom, chan + 1 - 2 * core)
    across = (dom, far)
    latent, count = nodes.shape
    own_rows = 2 * count
    halo_rows = reduced.shape[0]
    slots = halo_rows // parts
    halo_first = chans * own_rows

    def own_block(index):
        return pl.ds(pl.multiple_of(index * own_rows, own_rows), own_rows)

    def halo_block(index):
        return pl.ds(pl.multiple_of(halo_first + index * halo_rows, halo_rows), halo_rows)

    def push(src, dst, index, target):
        copy = pltpu.make_async_remote_copy(
            src_ref=src, dst_ref=dst, send_sem=send.at[index], recv_sem=recv.at[index],
            device_id=target, device_id_type=MESH,
        )
        copy.start()
        return copy

    columns = pl.ds(pl.multiple_of(chan * count, count), count)
    load = pltpu.make_async_copy(own.at[:, columns], nodes, local.at[0])
    load.start()
    enter(dom, chan, parts, chans)

    halo_pair = [push(sums.at[halo_block(2 * s + 1 - core), :], halo_in.at[s], s, sibling) for s in range(2)]
    own_pair = [push(sums.at[own_block(2 * s + 1 - core), :], own_in.at[s], 2 + s, sibling) for s in range(2)]
    for copy in halo_pair:
        copy.wait()
    halo_out[...] = (
        sums[halo_block(2 * other + core), :].astype(FLOAT) + halo_in[other].astype(FLOAT)
    ).astype(HALF)
    halo_cross = push(halo_out, halo_far, 4, across)
    for copy in own_pair:
        copy.wait()
    own_out[...] = (
        sums[own_block(2 * other + core), :].astype(FLOAT) + own_in[other].astype(FLOAT)
    ).astype(HALF)
    own_cross = push(own_out, own_far, 5, across)

    halo_cross.wait()
    reduced[...] = (
        sums[halo_block(chan), :].astype(FLOAT) + halo_in[side].astype(FLOAT) + halo_far[...].astype(FLOAT)
    ).astype(HALF)

    def send_part(k, carry):
        rows = pl.ds(pl.multiple_of(k * slots, slots), slots)
        pltpu.make_async_remote_copy(
            src_ref=reduced.at[rows, :], dst_ref=returned.at[chan, rows, :],
            send_sem=part_send, recv_sem=part_recv,
            device_id=(lax.rem(dom + 2 * parts - 1 - k, parts), chan), device_id_type=MESH,
        ).start()
        return carry

    lax.fori_loop(0, parts - 1, send_part, 0)
    last = pl.ds((parts - 1) * slots, slots)
    returned[chan, last, :] = reduced[last, :]

    tall = 128
    for start in range(0, count, tall):
        row = lax.broadcasted_iota(jnp.int32, (tall, 1), 0) + (start + chan * count)
        pick[pl.ds(start, tall), :] = jnp.where(rows_of[...] == row, 1.0, 0.0).astype(HALF)

    own_cross.wait()
    own_sum[...] = (
        sums[own_block(chan), :].astype(FLOAT) + own_in[side].astype(FLOAT) + own_far[...].astype(FLOAT)
    )

    arrived = returned.at[chan, pl.ds(0, (parts - 1) * slots), :]
    pltpu.make_async_copy(arrived, arrived, part_recv).wait()
    ring = [push(returned.at[chan], returned.at[chan], 6, across), push(returned.at[chan], returned.at[chan], 7, sibling)]
    ring[0].wait_recv()
    ring.append(push(returned.at[far], returned.at[far], 8, sibling))
    ring[1].wait()
    ring[2].wait()
    ring[0].wait_send()
    for c in range(chans):
        spread[pl.ds(c * halo_rows, halo_rows), :] = returned[c].astype(FLOAT)
    slot_total = chans * halo_rows // 2
    values = jnp.concatenate(
        [spread[pl.ds(0, slot_total, stride=2), :], spread[pl.ds(1, slot_total, stride=2), :]], axis=1
    ).astype(HALF)
    summed = jnp.concatenate([own_sum[pl.ds(0, count, stride=2), :], own_sum[pl.ds(1, count, stride=2), :]], axis=1)
    summed = summed + jnp.dot(pick[...], values, preferred_element_type=FLOAT)
    summed = summed.astype(HALF)

    load.wait()
    latents = nodes[...]
    pre = jnp.dot(w_in[:, :latent], latents, preferred_element_type=FLOAT)
    pre += lax.dot_general(
        w_in[:, latent:], summed, (((1,), (1,)), ((), ())), preferred_element_type=FLOAT
    )
    hidden = silu_rows(pre + vectors[:, 0:1]).astype(HALF)
    post = lax.dot_general(
        w_out[...], hidden, (((0,), (0,)), ((), ())), preferred_element_type=FLOAT
    ) + vectors[:, 3:4]
    centred = post - jnp.mean(post, axis=0, keepdims=True)
    var = jnp.mean(centred * centred, axis=0, keepdims=True)
    norm = centred * lax.rsqrt(var + 1e-05) * vectors[:, 1:2] + vectors[:, 2:3]
    fresh[...] = (latents.astype(FLOAT) + norm).astype(HALF)

    quarter = latent // chans

    def piece(index):
        return fresh.at[pl.ds(pl.multiple_of(index * quarter, quarter), quarter), :]

    keep = pltpu.make_async_copy(piece(chan), result.at[:, columns], local.at[1])
    keep.start()
    final = []
    for k in range(1, chans):
        to = lax.rem(chan + k, chans)
        final.append(push(piece(to), result.at[:, columns], 8 + k, (dom, to)))
    for copy in final:
        copy.wait()
    keep.wait()
    sent = reduced.at[pl.ds(0, (parts - 1) * slots), :]
    pltpu.make_async_copy(sent, sent, part_send).wait()


def reverse(sums, own, rows_of, w_in, w_out, vectors, parts, chans):
    latent, node_rows = own.shape
    count = node_rows // chans
    own_rows = 2 * count
    halo_rows = (sums.shape[0] - 2 * node_rows) // chans
    half = lambda *shape: pltpu.VMEM(shape, HALF)
    return pl.pallas_call(
        functools.partial(reverse_kernel, parts=parts, chans=chans),
        in_specs=[VMEM, ANY] + [VMEM] * 4,
        out_specs=VMEM,
        out_shape=jax.ShapeDtypeStruct((latent // chans, node_rows), HALF),
        scratch_shapes=[
            half(2, halo_rows, LANES), half(2, own_rows, LANES),
            half(halo_rows, LANES), half(own_rows, LANES),
            half(halo_rows, LANES), half(own_rows, LANES),
            half(halo_rows, LANES), half(chans, halo_rows, LANES),
            pltpu.VMEM((chans * halo_rows, LANES), FLOAT), pltpu.VMEM((own_rows, LANES), FLOAT),
            half(count, chans * halo_rows // 2), half(latent, count), half(latent, count),
            pltpu.SemaphoreType.DMA,
            pltpu.SemaphoreType.DMA,
            pltpu.SemaphoreType.DMA((12,)),
            pltpu.SemaphoreType.DMA((12,)),
            pltpu.SemaphoreType.DMA((2,)),
        ],
        compiler_params=pltpu.CompilerParams(
            collective_id=1, has_side_effects=True, vmem_limit_bytes=40 * 2**20
        ),
        name="reverse",
    )(sums, own, rows_of, w_in, w_out, vectors)


def body(
    node_latent,
    edge_latent,
    senders,
    receivers,
    edge_count,
    send_list,
    w_edge_in,
    edge_in_bias,
    w_edge_out,
    edge_out_bias,
    edge_gain,
    edge_shift,
    w_node_in,
    node_in_bias,
    w_node_out,
    node_out_bias,
    node_gain,
    node_shift,
):
    node_rows, quarter = node_latent.shape
    parts = lax.axis_size("dom")
    chans = lax.axis_size("chan")
    dom = lax.axis_index("dom")
    chan = lax.axis_index("chan")
    slots = send_list.shape[2]
    group = slots // chans
    edge_rows = edge_latent.shape[0]

    vectors = jnp.stack(
        [
            node_in_bias.astype(FLOAT), node_gain, node_shift,
            lax.dynamic_slice_in_dim(node_out_bias, chan * quarter, quarter, 0),
        ],
        axis=1,
    )
    vectors = jnp.pad(vectors, ((0, 0), (0, LANES - 4)))
    own, halo, all_in, all_out, all_vectors = forward(
        send_list[0].T, node_latent.T, w_node_in.T, w_node_out, vectors, parts, chans
    )

    slot = receivers - node_rows
    place = lax.rem(dom + 2 * parts - 1 - slot // slots, parts)
    slot = slot % slots
    halo_row = node_rows + (slot // group) * (parts * group) + place * group + slot % group
    rows = jnp.where(receivers < node_rows, receivers, halo_row)
    live = jnp.clip(edge_count - chan * edge_rows, 0, edge_rows)
    edge_new, sums = edge_block(
        senders, rows, live, own, halo, edge_latent, w_edge_in, edge_in_bias, w_edge_out,
        edge_out_bias, edge_gain, edge_shift,
    )

    order = lax.rem(dom + 1 + jnp.arange(parts, dtype=jnp.int32), parts)
    rows_of = send_list[0][order].reshape(parts, chans, group).transpose(1, 0, 2).reshape(1, parts * slots)
    node_new = reverse(sums, own, rows_of, all_in, all_out, all_vectors, parts, chans)
    return (node_new.T, edge_new)


def solution(mesh):
    placed = (
        P("dom", "chan"),
        P(("dom", "chan"), None),
        P(("dom", "chan")),
        P(("dom", "chan")),
        P("dom"),
        P("dom", None, None),
        P(),
        P(),
        P(),
        P(),
        P(),
        P(),
        P(None, "chan"),
        P("chan"),
        P("chan", None),
        P(),
        P("chan"),
        P("chan"),
    )
    return jax.shard_map(
        body,
        mesh=mesh,
        in_specs=placed,
        out_specs=(P("dom", "chan"), P(("dom", "chan"), None)),
        check_vma=False,
    )
```

```python
import functools

import jax
import jax.numpy as jnp
from jax import lax
from jax.experimental import pallas as pl
from jax.experimental.pallas import tpu as pltpu
from jax.sharding import PartitionSpec as P

LANES = 128
EDGE_TILE = 1344
UNROLL = 32
COPIES = 4
CHUNK = 512
GROUPS = 4
STEPS = 5
VMEM_LIMIT = 58 * 2**20
MESH = pl.DeviceIdType.MESH
FLOAT = jnp.float32
HALF = jnp.bfloat16
ANY = pl.BlockSpec(memory_space=pl.ANY)
VMEM = pl.BlockSpec(memory_space=pltpu.VMEM)


def silu_rows(values):
    return values * jax.nn.sigmoid(values)


def offset_of(place, parts):
    return 2 * lax.rem(place, parts // 2) + 1 + place // (parts // 2)


def enter(dom, chan, parts, chans):
    barrier = pltpu.get_barrier_semaphore()

    def greet(k, carry):
        offset = offset_of(k, parts)
        pl.semaphore_signal(
            barrier, inc=1,
            device_id=(lax.rem(dom + offset, parts), lax.rem(chan + 2 * (offset % 2), chans)),
            device_id_type=MESH,
        )
        return carry

    lax.fori_loop(0, parts - 1, greet, 0)
    for k in range(1, chans):
        pl.semaphore_signal(barrier, inc=1, device_id=(dom, lax.rem(chan + k, chans)), device_id_type=MESH)
    pl.semaphore_wait(barrier, parts + chans - 2)


def forward_kernel(
    send_rows, nodes, senders, receivers,
    own, halo, sender_rows, receiver_rows,
    wide, stage, outgoing, part_send, part_recv, send, recv, local,
    *, parts, chans,
):
    dom = lax.axis_index("dom")
    chan = lax.axis_index("chan")
    quarter, node_rows = nodes.shape
    slots = send_rows.shape[0] // 2
    half = parts // 2
    sibling = (dom, chan + 1 - 2 * lax.rem(chan, 2))
    far = lax.rem(chan + 2, chans)
    across = (dom, far)
    enter(dom, chan, parts, chans)

    def block(index):
        return own.at[pl.ds(pl.multiple_of(index * quarter, quarter), quarter), :]

    def push(src, dst, index, target):
        copy = pltpu.make_async_remote_copy(
            src_ref=src, dst_ref=dst, send_sem=send.at[index], recv_sem=recv.at[index],
            device_id=target, device_id_type=MESH,
        )
        copy.start()
        return copy

    crossed = push(nodes, block(chan), 0, across)
    done = [push(nodes, block(chan), 1, sibling)]
    keep = pltpu.make_async_copy(nodes, block(chan), local)
    keep.start()

    for start in range(0, node_rows, LANES):
        piece = nodes[:, start : start + LANES].astype(FLOAT)
        wide[pl.ds(start, LANES), :] = jnp.concatenate([piece, piece], axis=0).T

    left = lax.broadcasted_iota(jnp.int32, (1, LANES), 1) < quarter

    def fill(k):
        peer = lax.rem(dom + offset_of(k, parts), parts)
        base = pl.multiple_of(k * slots, slots)
        rows = []
        for j in range(slots):
            low = wide[pl.ds(send_rows[j, peer], 1), :]
            high = wide[pl.ds(send_rows[j + slots, peer], 1), :]
            rows.append(jnp.where(left, low, high))
        for j in range(slots):
            stage[pl.ds(base + j, 1), :] = rows[j]
        outgoing[k] = stage[pl.ds(base, slots), :].astype(HALF)
        return peer, base

    group = parts // GROUPS

    def send_part(k, carry):
        peer, base = fill(k)
        target = lax.rem(chan + 2 * (1 - k // half), chans)
        pltpu.make_async_remote_copy(
            src_ref=outgoing.at[k], dst_ref=halo.at[chan, pl.ds(base, slots), :],
            send_sem=part_send, recv_sem=part_recv.at[k // group],
            device_id=(peer, target), device_id_type=MESH,
        ).start()
        return carry

    lax.fori_loop(0, parts - 1, send_part, 0)
    _, base = fill(parts - 1)
    mine = pltpu.make_async_copy(
        outgoing.at[parts - 1], halo.at[chan, pl.ds(base, slots), :], part_recv.at[GROUPS - 1]
    )
    mine.start()

    sender_rows[...] = 2 * senders[...]
    index = receivers[...]
    slot = index - node_rows
    offset = (dom + 2 * parts - 1 - (slot >> 5)) & (parts - 1)
    place = (offset >> 1) + half * (offset & 1)
    halo_row = node_rows + ((slot >> 4) & 1) * (parts * slots) + place * slots + (slot & 15)
    receiver_rows[...] = 2 * jnp.where(index < node_rows, index, halo_row)

    crossed.wait_recv()
    done.append(push(block(far), block(far), 2, sibling))
    crossings = []
    for g in range(GROUPS):
        rows = pl.ds(g * group * slots, group * slots)
        here = far if g * group < half else chan
        piece = halo.at[here, rows, :]
        pltpu.make_async_copy(piece, piece, part_recv.at[g]).wait()
        crossings.append(push(piece, piece, 3 + 3 * g, across))
        done.append(push(piece, piece, 4 + 3 * g, sibling))
    for g in range(GROUPS):
        rows = pl.ds(g * group * slots, group * slots)
        there = chan if g * group < half else far
        piece = halo.at[there, rows, :]
        pltpu.make_async_remote_copy(
            src_ref=piece, dst_ref=piece, send_sem=send.at[3 + 3 * g], recv_sem=recv.at[3 + 3 * g],
            device_id=across, device_id_type=MESH,
        ).wait_recv()
        done.append(push(piece, piece, 5 + 3 * g, sibling))
    for copy in done:
        copy.wait()
    crossed.wait_send()
    for copy in crossings:
        copy.wait_send()
    keep.wait()
    sent = outgoing.at[pl.ds(0, parts - 1)]
    pltpu.make_async_copy(sent, sent, part_send).wait()


def forward(send_rows, nodes, senders, receivers, parts, chans):
    quarter, node_rows = nodes.shape
    slots = send_rows.shape[0]
    rows = parts * slots // 2
    copies = 3 * (1 + GROUPS)
    return pl.pallas_call(
        functools.partial(forward_kernel, parts=parts, chans=chans),
        in_specs=[pl.BlockSpec(memory_space=pltpu.SMEM)] + [VMEM] * 3,
        out_specs=[ANY] * 2 + [VMEM] * 2,
        out_shape=[
            jax.ShapeDtypeStruct((chans * quarter, node_rows), HALF),
            jax.ShapeDtypeStruct((chans, rows, LANES), HALF),
            jax.ShapeDtypeStruct(senders.shape, senders.dtype),
            jax.ShapeDtypeStruct(receivers.shape, receivers.dtype),
        ],
        scratch_shapes=[
            pltpu.VMEM((node_rows, LANES), FLOAT),
            pltpu.VMEM((rows, LANES), FLOAT),
            pltpu.VMEM((parts, slots // 2, LANES), HALF),
            pltpu.SemaphoreType.DMA,
            pltpu.SemaphoreType.DMA((GROUPS,)),
            pltpu.SemaphoreType.DMA((copies,)),
            pltpu.SemaphoreType.DMA((copies,)),
            pltpu.SemaphoreType.DMA,
        ],
        compiler_params=pltpu.CompilerParams(
            collective_id=0, has_side_effects=True, vmem_limit_bytes=VMEM_LIMIT
        ),
        name="forward",
    )(send_rows, nodes, senders, receivers)


def edge_kernel(
    senders, receivers, live, own, halo, edges, w_in, b_in, w_out, b_out, gain, shift,
    edge_new, sums, sent, received, gathered, messages, *partial,
):
    step = pl.program_id(0)
    tile, latent = edges.shape
    node_rows = own.shape[1]
    chans, halo_rows, _ = halo.shape
    quarter = latent // chans

    @pl.when(step == 0)
    def _():
        across = (((0,), (0,)), ((), ()))
        for start in range(0, node_rows, CHUNK):
            block = own[:, start : start + CHUNK]
            for target, first in ((sent, latent), (received, 2 * latent)):
                result = lax.dot_general(
                    block, w_in[first : first + latent, :], across, preferred_element_type=FLOAT
                )
                target[pl.ds(2 * start, CHUNK, stride=2), :] = result[:, :LANES]
                target[pl.ds(2 * start + 1, CHUNK, stride=2), :] = result[:, LANES:]
        weights = [w_in[2 * latent + c * quarter : 2 * latent + (c + 1) * quarter, :] for c in range(chans)]
        zero = jnp.zeros_like(weights[0])
        halves = []
        for side in range(2):
            padded = [[w, zero] if side == 0 else [zero, w] for w in weights]
            halves.append([
                jnp.concatenate(padded[c] + padded[c + 1], axis=0) for c in range(0, chans, 2)
            ])
        for start in range(0, halo_rows, CHUNK):
            blocks = [
                jnp.concatenate([halo[c, start : start + CHUNK, :], halo[c + 1, start : start + CHUNK, :]], axis=1)
                for c in range(0, chans, 2)
            ]
            for side in range(2):
                result = sum(
                    jnp.dot(b, w, preferred_element_type=FLOAT) for b, w in zip(blocks, halves[side])
                )
                at = 2 * (node_rows + side * halo_rows + start)
                received[pl.ds(at, CHUNK, stride=2), :] = result[:, :LANES]
                received[pl.ds(at + 1, CHUNK, stride=2), :] = result[:, LANES:]
        for part in partial:
            part[...] = jnp.zeros_like(part)

    base = step * tile

    def gather(k, carry):
        first = k * UNROLL
        rows = []
        for u in range(UNROLL):
            s = senders[base + first + u]
            r = receivers[base + first + u]
            rows.append(sent[pl.ds(s, 2), :] + received[pl.ds(r, 2), :])
        for u in range(UNROLL):
            gathered[pl.ds(2 * (first + u), 2), :] = rows[u]
        return carry

    lax.fori_loop(0, tile // UNROLL, gather, 0)

    latents = edges[...]
    pre = jnp.dot(latents, w_in[:latent, :], preferred_element_type=FLOAT)
    low = pre[:, :LANES] + gathered[pl.ds(0, tile, stride=2), :]
    high = pre[:, LANES:] + gathered[pl.ds(1, tile, stride=2), :]
    hidden = silu_rows(jnp.concatenate([low, high], axis=1) + b_in[...]).astype(HALF)
    post = jnp.dot(hidden, w_out[...], preferred_element_type=FLOAT) + b_out[...]
    centred = post - jnp.mean(post, axis=-1, keepdims=True)
    var = jnp.mean(centred * centred, axis=-1, keepdims=True)
    norm = centred * lax.rsqrt(var + 1e-05) * gain[...] + shift[...]
    row = lax.broadcasted_iota(jnp.int32, (tile, 1), 0) + base
    norm = jnp.where(row < live[0], norm, 0.0)
    new = (latents.astype(FLOAT) + norm).astype(HALF)
    edge_new[...] = new
    full = new.astype(FLOAT)
    messages[pl.ds(0, tile, stride=2), :] = full[:, :LANES]
    messages[pl.ds(1, tile, stride=2), :] = full[:, LANES:]

    def scatter(k, carry):
        first = k * UNROLL
        rows = [messages[pl.ds(2 * (first + u), 2), :] for u in range(UNROLL)]
        places = [pl.ds(receivers[base + first + u], 2) for u in range(UNROLL)]
        for start in range(0, UNROLL, COPIES):
            new_rows = [partial[u][places[start + u], :] + rows[start + u] for u in range(COPIES)]
            for u in range(COPIES):
                partial[u][places[start + u], :] = new_rows[u]
        return carry

    def scatter_one(j, carry):
        rows = pl.ds(receivers[base + j], 2)
        partial[0][rows, :] = partial[0][rows, :] + messages[pl.ds(2 * j, 2), :]
        return carry

    count = jnp.clip(live[0] - base, 0, tile)
    whole = count // UNROLL
    lax.fori_loop(0, whole, scatter, 0)
    lax.fori_loop(whole * UNROLL, count, scatter_one, 0)

    @pl.when(step == pl.num_programs(0) - 1)
    def _():
        table_rows = sums.shape[0] // 2

        def chunk(k, carry):
            start = pl.multiple_of(k * CHUNK, CHUNK)
            for lanes in range(2):
                rows = pl.ds(2 * start + lanes, CHUNK, stride=2)
                total = partial[0][rows, :]
                for part in partial[1:]:
                    total += part[rows, :]
                sums[pl.ds(lanes * table_rows + start, CHUNK), :] = total.astype(sums.dtype)
            return carry

        lax.fori_loop(0, table_rows // CHUNK, chunk, 0)


def edge_block(senders, receivers, live, own, halo, edges, w_in, b_in, w_out, b_out, gain, shift):
    edge_rows, latent = edges.shape
    node_rows = own.shape[1]
    table_rows = node_rows + 2 * halo.shape[1]
    tile = EDGE_TILE
    full = lambda array: pl.BlockSpec(array.shape, lambda i, *_: (0,) * array.ndim)
    tiled = pl.BlockSpec((tile, latent), lambda i, *_: (i, 0))
    scratch = lambda rows: pltpu.VMEM((2 * rows, LANES), FLOAT)
    b_in, b_out, gain, shift = (v.reshape(1, latent) for v in (b_in, b_out, gain, shift))
    return pl.pallas_call(
        edge_kernel,
        grid_spec=pltpu.PrefetchScalarGridSpec(
            num_scalar_prefetch=3,
            grid=(edge_rows // tile,),
            in_specs=[full(own), full(halo), tiled, full(w_in), full(b_in), full(w_out)] + [full(b_in)] * 3,
            out_specs=[tiled, pl.BlockSpec((2 * table_rows, LANES), lambda i, *_: (0, 0))],
            scratch_shapes=[scratch(node_rows), scratch(table_rows), scratch(tile), scratch(tile)]
            + [scratch(table_rows)] * COPIES,
        ),
        out_shape=[
            jax.ShapeDtypeStruct((edge_rows, latent), HALF),
            jax.ShapeDtypeStruct((2 * table_rows, LANES), HALF),
        ],
        compiler_params=pltpu.CompilerParams(vmem_limit_bytes=VMEM_LIMIT),
        name="edges",
    )(senders, receivers, live, own, halo, edges, w_in, b_in, w_out, b_out, gain, shift)


def reverse_kernel(
    sums, own, rows_of, w_in, w_out, vectors,
    result,
    halo_in, own_in, halo_mine, own_mine, halo_out, own_out, halo_far, own_far, reduced, returned,
    own_sum, pick, nodes, summed, fresh, all_in, all_out, all_vectors,
    part_send, part_recv, send, recv, local, row_send, row_recv,
    *, parts, chans,
):
    dom = lax.axis_index("dom")
    chan = lax.axis_index("chan")
    side = chan // 2
    core = lax.rem(chan, 2)
    half = lax.rem(side + dom, 2)
    other = 1 - half
    far = lax.rem(chan + 2, chans)
    sibling = (dom, chan + 1 - 2 * core)
    across = (dom, far)
    latent, count = nodes.shape
    quarter = latent // chans
    halo_rows = reduced.shape[0]
    slots = halo_rows // parts
    table_rows = sums.shape[0] // 2

    def own_block(lanes, index):
        return sums.at[pl.ds(pl.multiple_of(lanes * table_rows + index * count, LANES), count), :]

    def halo_block(lanes, index):
        start = pl.multiple_of(lanes * table_rows + 2 * count + index * halo_rows, LANES)
        return sums.at[pl.ds(start, halo_rows), :]

    def push(src, dst, index, target):
        copy = pltpu.make_async_remote_copy(
            src_ref=src, dst_ref=dst, send_sem=send.at[index], recv_sem=recv.at[index],
            device_id=target, device_id_type=MESH,
        )
        copy.start()
        return copy

    def fetch(src, dst, index):
        copy = pltpu.make_async_copy(src, dst, local.at[index])
        copy.start()
        return copy

    columns = pl.ds(pl.multiple_of(core * count, count), count)
    halo_mine_in = [fetch(halo_block(s, core), halo_mine.at[s], s) for s in range(2)]
    own_mine_in = [fetch(own_block(s, core), own_mine.at[s], 2 + s) for s in range(2)]
    load = fetch(own.at[:, columns], nodes, 4)
    enter(dom, chan, parts, chans)

    halo_pair = [push(halo_block(s, 1 - core), halo_in.at[s], s, sibling) for s in range(2)]
    own_pair = [push(own_block(s, 1 - core), own_in.at[s], 2 + s, sibling) for s in range(2)]
    weights = [(w_in, all_in), (w_out, all_out), (vectors, all_vectors)]
    weight_crossed, weight_done = [], []
    for n, (src, dst) in enumerate(weights):
        weight_crossed.append(push(src, dst.at[chan], 6 + 3 * n, across))
        weight_done.append(push(src, dst.at[chan], 7 + 3 * n, sibling))
        dst[chan] = src[...]

    for copy in halo_mine_in + halo_pair:
        copy.wait()
    halo_out[...] = (halo_mine[other].astype(FLOAT) + halo_in[other].astype(FLOAT)).astype(HALF)
    halo_cross = push(halo_out, halo_far, 4, across)
    for copy in own_mine_in + own_pair:
        copy.wait()
    own_out[...] = (own_mine[other].astype(FLOAT) + own_in[other].astype(FLOAT)).astype(HALF)
    own_cross = push(own_out, own_far, 5, across)

    halo_cross.wait()
    reduced[...] = (
        halo_mine[half].astype(FLOAT) + halo_in[half].astype(FLOAT) + halo_far[...].astype(FLOAT)
    ).astype(HALF)

    def send_part(k, carry):
        offset = offset_of(k, parts)
        rows = pl.ds(pl.multiple_of(k * slots, slots), slots)
        pltpu.make_async_remote_copy(
            src_ref=reduced.at[rows, :], dst_ref=returned.at[core, rows, :],
            send_sem=part_send, recv_sem=part_recv.at[k // (parts // GROUPS)],
            device_id=(lax.rem(dom + parts - offset, parts), lax.rem(chan + 2 * (offset % 2), chans)),
            device_id_type=MESH,
        ).start()
        return carry

    lax.fori_loop(0, parts - 1, send_part, 0)
    last = pl.ds((parts - 1) * slots, slots)
    mine = pltpu.make_async_copy(reduced.at[last, :], returned.at[core, last, :], part_recv.at[GROUPS - 1])
    mine.start()

    def choose(n, carry):
        start = pl.multiple_of(n * LANES, LANES)
        row = lax.broadcasted_iota(jnp.int32, (LANES, 1), 0) + (start + core * count)
        pick[pl.ds(start, LANES), :] = jnp.where(rows_of[...] == row, 1.0, 0.0).astype(HALF)
        return carry

    lax.fori_loop(0, count // LANES, choose, 0)

    for n, (src, dst) in enumerate(weights):
        weight_crossed[n].wait()
        weight_done.append(push(dst.at[far], dst.at[far], 8 + 3 * n, sibling))

    own_cross.wait()
    own_sum[...] = own_mine[half].astype(FLOAT) + own_in[half].astype(FLOAT) + own_far[...].astype(FLOAT)

    group_rows = halo_rows // GROUPS
    pairs = []
    for g in range(GROUPS):
        rows = pl.ds(g * group_rows, group_rows)
        piece = returned.at[core, rows, :]
        pltpu.make_async_copy(piece, piece, part_recv.at[g]).wait()
        pairs.append(push(piece, piece, 15 + g, sibling))
    for copy in pairs + weight_done:
        copy.wait()

    values = returned[...].reshape(2 * halo_rows, LANES)
    pieces = range(0, count, count // STEPS)
    sent = []
    for n, start in enumerate(pieces):
        rows = pl.ds(start, count // STEPS)
        total = own_sum[rows, :] + jnp.dot(pick[rows, :], values, preferred_element_type=FLOAT)
        summed[half, rows, :] = total.astype(HALF)
        piece = summed.at[half, rows, :]
        copy = pltpu.make_async_remote_copy(
            src_ref=piece, dst_ref=piece, send_sem=row_send.at[n], recv_sem=row_recv.at[n],
            device_id=across, device_id_type=MESH,
        )
        copy.start()
        sent.append(copy)

    load.wait()
    first_layer = all_in[...].reshape(latent, 2 * latent)
    second_layer = all_out[...].reshape(latent, latent)
    vector = all_vectors[...].reshape(latent, LANES)
    both = (((1,), (1,)), ((), ()))
    for n, start in enumerate(pieces):
        rows = pl.ds(start, count // STEPS)
        latents = nodes[:, rows]
        pre = jnp.dot(first_layer[:, :latent], latents, preferred_element_type=FLOAT)
        piece = summed.at[other, rows, :]
        pltpu.make_async_remote_copy(
            src_ref=piece, dst_ref=piece, send_sem=row_send.at[n], recv_sem=row_recv.at[n],
            device_id=across, device_id_type=MESH,
        ).wait_recv()
        total = jnp.concatenate([summed[0, rows, :], summed[1, rows, :]], axis=1)
        pre += lax.dot_general(first_layer[:, latent:], total, both, preferred_element_type=FLOAT)
        hidden = silu_rows(pre + vector[:, 0:1]).astype(HALF)
        post = lax.dot_general(
            second_layer, hidden, (((0,), (0,)), ((), ())), preferred_element_type=FLOAT
        ) + vector[:, 3:4]
        centred = post - jnp.mean(post, axis=0, keepdims=True)
        var = jnp.mean(centred * centred, axis=0, keepdims=True)
        norm = centred * lax.rsqrt(var + 1e-05) * vector[:, 1:2] + vector[:, 2:3]
        new = (latents.astype(FLOAT) + norm).astype(HALF)
        for c in range(chans):
            fresh[c, :, rows] = new[c * quarter : (c + 1) * quarter, :]

    keep = fetch(fresh.at[chan], result.at[:, columns], 5)
    final = push(fresh.at[chan + 1 - 2 * core], result.at[:, columns], 19, sibling)
    for copy in sent:
        copy.wait_send()
    gone = reduced.at[pl.ds(0, (parts - 1) * slots), :]
    pltpu.make_async_copy(gone, gone, part_send).wait()
    keep.wait()
    final.wait()


def reverse(sums, own, rows_of, w_in, w_out, vectors, parts, chans):
    latent, node_rows = own.shape
    count = node_rows // 2
    halo_rows = (sums.shape[0] - 2 * node_rows) // 4
    half = lambda *shape: pltpu.VMEM(shape, HALF)
    return pl.pallas_call(
        functools.partial(reverse_kernel, parts=parts, chans=chans),
        in_specs=[ANY, ANY] + [VMEM] * 4,
        out_specs=VMEM,
        out_shape=jax.ShapeDtypeStruct((latent // chans, node_rows), HALF),
        scratch_shapes=[
            half(2, halo_rows, LANES), half(2, count, LANES),
            half(2, halo_rows, LANES), half(2, count, LANES),
            half(halo_rows, LANES), half(count, LANES),
            half(halo_rows, LANES), half(count, LANES),
            half(halo_rows, LANES), half(2, halo_rows, LANES),
            pltpu.VMEM((count, LANES), FLOAT),
            half(count, 2 * halo_rows), half(latent, count), half(2, count, LANES),
            half(chans, latent // chans, count),
            half(chans, *w_in.shape), half(chans, *w_out.shape), pltpu.VMEM((chans, *vectors.shape), FLOAT),
            pltpu.SemaphoreType.DMA,
            pltpu.SemaphoreType.DMA((GROUPS,)),
            pltpu.SemaphoreType.DMA((20,)),
            pltpu.SemaphoreType.DMA((20,)),
            pltpu.SemaphoreType.DMA((6,)),
            pltpu.SemaphoreType.DMA((STEPS,)),
            pltpu.SemaphoreType.DMA((STEPS,)),
        ],
        compiler_params=pltpu.CompilerParams(
            collective_id=1, has_side_effects=True, vmem_limit_bytes=VMEM_LIMIT
        ),
        name="reverse",
    )(sums, own, rows_of, w_in, w_out, vectors)


def body(
    node_latent,
    edge_latent,
    senders,
    receivers,
    edge_count,
    send_list,
    w_edge_in,
    edge_in_bias,
    w_edge_out,
    edge_out_bias,
    edge_gain,
    edge_shift,
    w_node_in,
    node_in_bias,
    w_node_out,
    node_out_bias,
    node_gain,
    node_shift,
):
    node_rows, quarter = node_latent.shape
    parts = lax.axis_size("dom")
    chans = lax.axis_size("chan")
    dom = lax.axis_index("dom")
    chan = lax.axis_index("chan")
    slots = send_list.shape[2]
    edge_rows = edge_latent.shape[0]

    vectors = jnp.stack(
        [
            node_in_bias.astype(FLOAT), node_gain, node_shift,
            lax.dynamic_slice_in_dim(node_out_bias, chan * quarter, quarter, 0),
        ],
        axis=1,
    )
    vectors = jnp.pad(vectors, ((0, 0), (0, LANES - 4)))
    own, halo, sender_rows, receiver_rows = forward(
        send_list[0].T, node_latent.T, senders.reshape(-1, LANES), receivers.reshape(-1, LANES), parts, chans
    )
    live = jnp.clip(edge_count - chan * edge_rows, 0, edge_rows)
    edge_new, sums = edge_block(
        sender_rows.reshape(-1), receiver_rows.reshape(-1), live, own, halo, edge_latent, w_edge_in,
        edge_in_bias, w_edge_out, edge_out_bias, edge_gain, edge_shift,
    )

    source = lax.rem(dom + offset_of(jnp.arange(parts, dtype=jnp.int32), parts), parts)
    rows_of = send_list[0][source].reshape(parts, 2, slots // 2).transpose(1, 0, 2).reshape(1, parts * slots)
    node_new = reverse(sums, own, rows_of, w_node_in.T, w_node_out, vectors, parts, chans)
    return (node_new.T, edge_new)


def solution(mesh):
    placed = (
        P("dom", "chan"),
        P(("dom", "chan"), None),
        P(("dom", "chan")),
        P(("dom", "chan")),
        P("dom"),
        P("dom", None, None),
        P(),
        P(),
        P(),
        P(),
        P(),
        P(),
        P(None, "chan"),
        P("chan"),
        P("chan", None),
        P(),
        P("chan"),
        P("chan"),
    )
    return jax.shard_map(
        body,
        mesh=mesh,
        in_specs=placed,
        out_specs=(P("dom", "chan"), P(("dom", "chan"), None)),
        check_vma=False,
    )
```

```python
import functools

import jax
import jax.numpy as jnp
from jax import lax
from jax.experimental import pallas as pl
from jax.experimental.pallas import tpu as pltpu
from jax.sharding import PartitionSpec as P

LANES = 128
EDGE_TILE = 1344
UNROLL = 32
COPIES = 4
CHUNK = 512
GROUPS = 4
STEPS = 5
VMEM_LIMIT = 58 * 2**20
MESH = pl.DeviceIdType.MESH
FLOAT = jnp.float32
HALF = jnp.bfloat16
ANY = pl.BlockSpec(memory_space=pl.ANY)
VMEM = pl.BlockSpec(memory_space=pltpu.VMEM)


def silu_rows(values):
    return values * jax.nn.sigmoid(values)


def offset_of(place, parts):
    return 2 * lax.rem(place, parts // 2) + 1 + place // (parts // 2)


def enter(dom, chan, parts, chans):
    barrier = pltpu.get_barrier_semaphore()

    def greet(k, carry):
        offset = offset_of(k, parts)
        pl.semaphore_signal(
            barrier, inc=1,
            device_id=(lax.rem(dom + offset, parts), lax.rem(chan + 2 * (offset % 2), chans)),
            device_id_type=MESH,
        )
        return carry

    lax.fori_loop(0, parts - 1, greet, 0)
    for k in range(1, chans):
        pl.semaphore_signal(barrier, inc=1, device_id=(dom, lax.rem(chan + k, chans)), device_id_type=MESH)
    pl.semaphore_wait(barrier, parts + chans - 2)


def forward_kernel(
    send_rows, nodes, senders, receivers,
    own, halo, sender_rows, receiver_rows,
    wide, stage, outgoing, part_send, part_recv, send, recv, local,
    *, parts, chans,
):
    dom = lax.axis_index("dom")
    chan = lax.axis_index("chan")
    quarter, node_rows = nodes.shape
    slots = send_rows.shape[0] // 2
    half = parts // 2
    sibling = (dom, chan + 1 - 2 * lax.rem(chan, 2))
    far = lax.rem(chan + 2, chans)
    across = (dom, far)
    enter(dom, chan, parts, chans)

    def block(index, n):
        rows = pl.ds(pl.multiple_of(index * quarter, quarter), quarter)
        return own.at[rows, n * node_rows // STEPS : (n + 1) * node_rows // STEPS]

    def push(src, dst, index, target):
        copy = pltpu.make_async_remote_copy(
            src_ref=src, dst_ref=dst, send_sem=send.at[index], recv_sem=recv.at[index],
            device_id=target, device_id_type=MESH,
        )
        copy.start()
        return copy

    crossed, done = [], []

    def push_own(n):
        piece = nodes.at[:, n * node_rows // STEPS : (n + 1) * node_rows // STEPS]
        crossed.append(push(piece, block(chan, n), 3 * (GROUPS + n), across))
        done.append(push(piece, block(chan, n), 3 * (GROUPS + n) + 1, sibling))

    rows = pl.ds(pl.multiple_of(chan * quarter, quarter), quarter)
    keep = pltpu.make_async_copy(nodes, own.at[rows, :], local)
    keep.start()
    for n in range(STEPS):
        push_own(n)

    for start in range(0, node_rows, LANES):
        piece = nodes[:, start : start + LANES].astype(FLOAT)
        wide[pl.ds(start, LANES), :] = jnp.concatenate([piece, piece], axis=0).T

    left = lax.broadcasted_iota(jnp.int32, (1, LANES), 1) < quarter

    def fill(k):
        peer = lax.rem(dom + offset_of(k, parts), parts)
        base = pl.multiple_of(k * slots, slots)
        rows = []
        for j in range(slots):
            low = wide[pl.ds(send_rows[j, peer], 1), :]
            high = wide[pl.ds(send_rows[j + slots, peer], 1), :]
            rows.append(jnp.where(left, low, high))
        for j in range(slots):
            stage[pl.ds(base + j, 1), :] = rows[j]
        outgoing[k] = stage[pl.ds(base, slots), :].astype(HALF)
        return peer, base

    group = parts // GROUPS

    def send_part(k, carry):
        peer, base = fill(k)
        target = lax.rem(chan + 2 * (1 - k // half), chans)
        pltpu.make_async_remote_copy(
            src_ref=outgoing.at[k], dst_ref=halo.at[chan, pl.ds(base, slots), :],
            send_sem=part_send, recv_sem=part_recv.at[k // group],
            device_id=(peer, target), device_id_type=MESH,
        ).start()
        return carry

    crossings, pieces = [], []

    def share(g):
        rows = pl.ds(g * group * slots, group * slots)
        here, there = (far, chan) if g * group < half else (chan, far)
        piece = halo.at[here, rows, :]
        pltpu.make_async_copy(piece, piece, part_recv.at[g]).wait()
        crossings.append(push(piece, piece, 3 * g, across))
        done.append(push(piece, piece, 1 + 3 * g, sibling))
        pieces.append(halo.at[there, rows, :])

    for g in range(GROUPS):
        lax.fori_loop(g * group, min((g + 1) * group, parts - 1), send_part, 0)
    _, base = fill(parts - 1)
    mine = pltpu.make_async_copy(
        outgoing.at[parts - 1], halo.at[chan, pl.ds(base, slots), :], part_recv.at[GROUPS - 1]
    )
    mine.start()

    sender_rows[...] = 2 * senders[...]
    index = receivers[...]
    slot = index - node_rows
    offset = (dom + 2 * parts - 1 - (slot >> 5)) & (parts - 1)
    place = (offset >> 1) + half * (offset & 1)
    halo_row = node_rows + ((slot >> 4) & 1) * (parts * slots) + place * slots + (slot & 15)
    receiver_rows[...] = 2 * jnp.where(index < node_rows, index, halo_row)

    for g in range(GROUPS):
        share(g)
    for n in range(STEPS):
        crossed[n].wait_recv()
        done.append(push(block(far, n), block(far, n), 3 * (GROUPS + n) + 2, sibling))
    for g, piece in enumerate(pieces):
        pltpu.make_async_remote_copy(
            src_ref=piece, dst_ref=piece, send_sem=send.at[3 * g], recv_sem=recv.at[3 * g],
            device_id=across, device_id_type=MESH,
        ).wait_recv()
        done.append(push(piece, piece, 2 + 3 * g, sibling))
    for copy in done:
        copy.wait()
    for copy in crossed:
        copy.wait_send()
    for copy in crossings:
        copy.wait_send()
    keep.wait()
    sent = outgoing.at[pl.ds(0, parts - 1)]
    pltpu.make_async_copy(sent, sent, part_send).wait()


def forward(send_rows, nodes, senders, receivers, parts, chans):
    quarter, node_rows = nodes.shape
    slots = send_rows.shape[0]
    rows = parts * slots // 2
    copies = 3 * (STEPS + GROUPS)
    return pl.pallas_call(
        functools.partial(forward_kernel, parts=parts, chans=chans),
        in_specs=[pl.BlockSpec(memory_space=pltpu.SMEM)] + [VMEM] * 3,
        out_specs=[ANY] * 2 + [VMEM] * 2,
        out_shape=[
            jax.ShapeDtypeStruct((chans * quarter, node_rows), HALF),
            jax.ShapeDtypeStruct((chans, rows, LANES), HALF),
            jax.ShapeDtypeStruct(senders.shape, senders.dtype),
            jax.ShapeDtypeStruct(receivers.shape, receivers.dtype),
        ],
        scratch_shapes=[
            pltpu.VMEM((node_rows, LANES), FLOAT),
            pltpu.VMEM((rows, LANES), FLOAT),
            pltpu.VMEM((parts, slots // 2, LANES), HALF),
            pltpu.SemaphoreType.DMA,
            pltpu.SemaphoreType.DMA((GROUPS,)),
            pltpu.SemaphoreType.DMA((copies,)),
            pltpu.SemaphoreType.DMA((copies,)),
            pltpu.SemaphoreType.DMA,
        ],
        compiler_params=pltpu.CompilerParams(
            collective_id=0, has_side_effects=True, vmem_limit_bytes=VMEM_LIMIT
        ),
        name="forward",
    )(send_rows, nodes, senders, receivers)


def edge_kernel(
    live, senders_in, receivers_in, own_in, halo_in, edges_in, w_in_in, b_in, w_out, b_out, gain, shift,
    edge_new, sums,
    senders, receivers, own, halo, edges, w_in, fresh, totals, sent, received, gathered, messages, loads, tile_out, sum_out,
    *partial,
):
    tile = messages.shape[0] // 2
    edge_rows, latent = edges.shape
    node_rows = own.shape[1]
    chans, halo_rows, _ = halo.shape
    quarter = latent // chans
    steps = edge_rows // tile

    loading = []
    for n, (src, dst) in enumerate((
        (own_in, own), (w_in_in, w_in), (halo_in, halo), (senders_in, senders), (receivers_in, receivers), (edges_in, edges)
    )):
        loading.append(pltpu.make_async_copy(src, dst, loads.at[n]))
        loading[-1].start()
    for part in partial:
        part[...] = jnp.zeros_like(part)
    loading[0].wait()
    loading[1].wait()
    across = (((0,), (0,)), ((), ()))
    for start in range(0, node_rows, CHUNK):
        block = own[:, start : start + CHUNK]
        for target, first in ((sent, latent), (received, 2 * latent)):
            result = lax.dot_general(
                block, w_in[first : first + latent, :], across, preferred_element_type=FLOAT
            )
            target[pl.ds(2 * start, CHUNK, stride=2), :] = result[:, :LANES]
            target[pl.ds(2 * start + 1, CHUNK, stride=2), :] = result[:, LANES:]
    weights = [w_in[2 * latent + c * quarter : 2 * latent + (c + 1) * quarter, :] for c in range(chans)]
    zero = jnp.zeros_like(weights[0])
    halves = []
    for side in range(2):
        padded = [[w, zero] if side == 0 else [zero, w] for w in weights]
        halves.append([
            jnp.concatenate(padded[c] + padded[c + 1], axis=0) for c in range(0, chans, 2)
        ])
    loading[2].wait()
    for start in range(0, halo_rows, CHUNK):
        blocks = [
            jnp.concatenate([halo[c, start : start + CHUNK, :], halo[c + 1, start : start + CHUNK, :]], axis=1)
            for c in range(0, chans, 2)
        ]
        for side in range(2):
            result = sum(
                jnp.dot(b, w, preferred_element_type=FLOAT) for b, w in zip(blocks, halves[side])
            )
            at = 2 * (node_rows + side * halo_rows + start)
            received[pl.ds(at, CHUNK, stride=2), :] = result[:, :LANES]
            received[pl.ds(at + 1, CHUNK, stride=2), :] = result[:, LANES:]
    for copy in loading[3:]:
        copy.wait()

    def one_tile(step, carry):
        base = pl.multiple_of(step * tile, tile)

        def gather(k, carry):
            first = k * UNROLL
            rows = []
            for u in range(UNROLL):
                s = senders[base + first + u]
                r = receivers[base + first + u]
                rows.append(sent[pl.ds(s, 2), :] + received[pl.ds(r, 2), :])
            for u in range(UNROLL):
                gathered[pl.ds(2 * (first + u), 2), :] = rows[u]
            return carry

        lax.fori_loop(0, tile // UNROLL, gather, 0)

        latents = edges[pl.ds(base, tile), :]
        pre = jnp.dot(latents, w_in[:latent, :], preferred_element_type=FLOAT)
        low = pre[:, :LANES] + gathered[pl.ds(0, tile, stride=2), :]
        high = pre[:, LANES:] + gathered[pl.ds(1, tile, stride=2), :]
        hidden = silu_rows(jnp.concatenate([low, high], axis=1) + b_in[...]).astype(HALF)
        post = jnp.dot(hidden, w_out[...], preferred_element_type=FLOAT) + b_out[...]
        centred = post - jnp.mean(post, axis=-1, keepdims=True)
        var = jnp.mean(centred * centred, axis=-1, keepdims=True)
        norm = centred * lax.rsqrt(var + 1e-05) * gain[...] + shift[...]
        row = lax.broadcasted_iota(jnp.int32, (tile, 1), 0) + base
        norm = jnp.where(row < live[0], norm, 0.0)
        new = (latents.astype(FLOAT) + norm).astype(HALF)
        fresh[pl.ds(base, tile), :] = new
        pltpu.make_async_copy(
            fresh.at[pl.ds(base, tile), :], edge_new.at[pl.ds(base, tile), :], tile_out
        ).start()
        full = new.astype(FLOAT)
        messages[pl.ds(0, tile, stride=2), :] = full[:, :LANES]
        messages[pl.ds(1, tile, stride=2), :] = full[:, LANES:]

        def scatter(k, carry):
            first = k * UNROLL
            rows = [messages[pl.ds(2 * (first + u), 2), :] for u in range(UNROLL)]
            places = [pl.ds(receivers[base + first + u], 2) for u in range(UNROLL)]
            for start in range(0, UNROLL, COPIES):
                new_rows = [partial[u][places[start + u], :] + rows[start + u] for u in range(COPIES)]
                for u in range(COPIES):
                    partial[u][places[start + u], :] = new_rows[u]
            return carry

        def scatter_one(j, carry):
            rows = pl.ds(receivers[base + j], 2)
            partial[0][rows, :] = partial[0][rows, :] + messages[pl.ds(2 * j, 2), :]
            return carry

        count = jnp.clip(live[0] - base, 0, tile)
        whole = count // UNROLL
        lax.fori_loop(0, whole, scatter, 0)
        lax.fori_loop(whole * UNROLL, count, scatter_one, 0)
        return carry

    lax.fori_loop(0, steps, one_tile, 0)

    table_rows = sums.shape[0] // 2
    pieces = 3
    piece_rows = table_rows // pieces

    def total_chunk(k, carry):
        start = pl.multiple_of(k * CHUNK, CHUNK)
        for lanes in range(2):
            rows = pl.ds(2 * start + lanes, CHUNK, stride=2)
            total = partial[0][rows, :]
            for part in partial[1:]:
                total += part[rows, :]
            totals[pl.ds(lanes * table_rows + start, CHUNK), :] = total.astype(sums.dtype)
        return carry

    leaving = []
    for n in range(pieces):
        chunks = piece_rows // CHUNK
        lax.fori_loop(n * chunks, (n + 1) * chunks, total_chunk, 0)
        for lanes in range(2):
            rows = pl.ds(lanes * table_rows + n * piece_rows, piece_rows)
            leaving.append(pltpu.make_async_copy(totals.at[rows, :], sums.at[rows, :], sum_out.at[2 * n + lanes]))
            leaving[-1].start()
    for copy in leaving:
        copy.wait()
    pltpu.make_async_copy(fresh, edge_new, tile_out).wait()


def edge_block(senders, receivers, live, own, halo, edges, w_in, b_in, w_out, b_out, gain, shift):
    edge_rows, latent = edges.shape
    node_rows = own.shape[1]
    table_rows = node_rows + 2 * halo.shape[1]
    scratch = lambda rows: pltpu.VMEM((2 * rows, LANES), FLOAT)
    like = lambda array: pltpu.VMEM(array.shape, array.dtype)
    b_in, b_out, gain, shift = (v.reshape(1, latent) for v in (b_in, b_out, gain, shift))
    return pl.pallas_call(
        edge_kernel,
        in_specs=[pl.BlockSpec(memory_space=pltpu.SMEM)] + [ANY] * 6 + [VMEM] * 5,
        out_specs=[ANY] * 2,
        scratch_shapes=[
            pltpu.SMEM(senders.shape, senders.dtype), pltpu.SMEM(receivers.shape, receivers.dtype),
            like(own), like(halo), like(edges), like(w_in), like(edges), pltpu.VMEM((2 * table_rows, LANES), HALF),
            scratch(node_rows), scratch(table_rows), scratch(EDGE_TILE), scratch(EDGE_TILE),
            pltpu.SemaphoreType.DMA((6,)), pltpu.SemaphoreType.DMA, pltpu.SemaphoreType.DMA((6,)),
        ] + [scratch(table_rows)] * COPIES,
        out_shape=[
            jax.ShapeDtypeStruct((edge_rows, latent), HALF),
            jax.ShapeDtypeStruct((2 * table_rows, LANES), HALF),
        ],
        compiler_params=pltpu.CompilerParams(vmem_limit_bytes=VMEM_LIMIT),
        name="edges",
    )(live, senders, receivers, own, halo, edges, w_in, b_in, w_out, b_out, gain, shift)


def reverse_kernel(
    sums, own, rows_of, w_in, w_out, in_bias, out_bias, gain, shift,
    result,
    halo_in, own_in, halo_mine, own_mine, halo_out, own_out, halo_far, own_far, reduced, returned,
    pick, nodes, summed, fresh, vectors, all_in, all_out, all_vectors,
    part_send, part_recv, send, recv, local, halo_send, halo_recv, own_send, own_recv, row_send, row_recv,
    end_send, end_recv, end_local,
    *, parts, chans,
):
    dom = lax.axis_index("dom")
    chan = lax.axis_index("chan")
    side = chan // 2
    core = lax.rem(chan, 2)
    half = lax.rem(side + dom, 2)
    other = 1 - half
    far = lax.rem(chan + 2, chans)
    sibling = (dom, chan + 1 - 2 * core)
    across = (dom, far)
    latent, count = nodes.shape
    quarter = latent // chans
    halo_rows = reduced.shape[0]
    slots = halo_rows // parts
    table_rows = sums.shape[0] // 2

    def own_block(lanes, index):
        return sums.at[pl.ds(pl.multiple_of(lanes * table_rows + index * count, LANES), count), :]

    def halo_block(lanes, index):
        start = pl.multiple_of(lanes * table_rows + 2 * count + index * halo_rows, LANES)
        return sums.at[pl.ds(start, halo_rows), :]

    def describe(src, dst, sends, recvs, index, target):
        return pltpu.make_async_remote_copy(
            src_ref=src, dst_ref=dst, send_sem=sends.at[index], recv_sem=recvs.at[index],
            device_id=target, device_id_type=MESH,
        )

    def push(*where):
        copy = describe(*where)
        copy.start()
        return copy

    def fetch(src, dst, sems, index):
        copy = pltpu.make_async_copy(src, dst, sems.at[index])
        copy.start()
        return copy

    columns = pl.ds(pl.multiple_of(core * count, count), count)
    mine = [
        fetch(halo_block(other, core), halo_mine.at[other], local, 0),
        fetch(own_block(other, core), own_mine.at[other], local, 1),
        fetch(halo_block(half, core), halo_mine.at[half], local, 2),
        fetch(own_block(half, core), own_mine.at[half], local, 3),
    ]
    load = fetch(own.at[:, columns], nodes, local, 4)
    vectors[...] = jnp.zeros_like(vectors)
    for n, values in enumerate((in_bias, gain, shift)):
        vectors[n : n + 1, :quarter] = values[...].astype(FLOAT)
    enter(dom, chan, parts, chans)

    pair = [
        push(halo_block(other, 1 - core), halo_in.at[other], send, recv, 0, sibling),
        push(own_block(other, 1 - core), own_in.at[other], send, recv, 1, sibling),
        push(halo_block(half, 1 - core), halo_in.at[half], send, recv, 2, sibling),
        push(own_block(half, 1 - core), own_in.at[half], send, recv, 3, sibling),
    ]
    weights = [(w_in, all_in), (w_out, all_out), (vectors, all_vectors)]
    weight_crossed, weight_done = [], []
    for n, (src, dst) in enumerate(weights):
        weight_crossed.append(push(src, dst.at[chan], send, recv, 4 + 3 * n, across))
        weight_done.append(push(src, dst.at[chan], send, recv, 5 + 3 * n, sibling))
        dst[chan] = src[...]

    group_rows = halo_rows // GROUPS
    step_rows = count // STEPS
    mine[0].wait()
    pair[0].wait()
    halo_cross, own_cross = [], []
    for g in range(GROUPS):
        rows = pl.ds(g * group_rows, group_rows)
        halo_out[rows, :] = (
            halo_mine[other, rows, :].astype(FLOAT) + halo_in[other, rows, :].astype(FLOAT)
        ).astype(HALF)
        halo_cross.append(push(halo_out.at[rows, :], halo_far.at[rows, :], halo_send, halo_recv, g, across))
    mine[1].wait()
    pair[1].wait()
    for n in range(STEPS):
        rows = pl.ds(n * step_rows, step_rows)
        own_out[rows, :] = (
            own_mine[other, rows, :].astype(FLOAT) + own_in[other, rows, :].astype(FLOAT)
        ).astype(HALF)
        own_cross.append(push(own_out.at[rows, :], own_far.at[rows, :], own_send, own_recv, n, across))

    def send_part(k, carry):
        offset = offset_of(k, parts)
        rows = pl.ds(pl.multiple_of(k * slots, slots), slots)
        landing = pl.ds(pl.multiple_of(dom * slots, slots), slots)
        pltpu.make_async_remote_copy(
            src_ref=reduced.at[rows, :], dst_ref=returned.at[core, landing, :],
            send_sem=part_send, recv_sem=part_recv,
            device_id=(lax.rem(dom + parts - offset, parts), lax.rem(chan + 2 * (offset % 2), chans)),
            device_id_type=MESH,
        ).start()
        return carry

    mine[2].wait()
    pair[2].wait()
    group = parts // GROUPS
    for g in range(GROUPS):
        rows = pl.ds(g * group_rows, group_rows)
        halo_cross[g].wait()
        reduced[rows, :] = (
            halo_mine[half, rows, :].astype(FLOAT)
            + halo_in[half, rows, :].astype(FLOAT)
            + halo_far[rows, :].astype(FLOAT)
        ).astype(HALF)
        lax.fori_loop(g * group, min((g + 1) * group, parts - 1), send_part, 0)
    last = pl.ds((parts - 1) * slots, slots)
    landing = pl.ds(pl.multiple_of(dom * slots, slots), slots)
    pltpu.make_async_copy(reduced.at[last, :], returned.at[core, landing, :], part_recv).start()

    def choose(n, carry):
        start = pl.multiple_of(n * LANES, LANES)
        row = lax.broadcasted_iota(jnp.int32, (LANES, 1), 0) + (start + core * count)
        pick[pl.ds(start, LANES), :] = jnp.where(rows_of[...] == row, 1.0, 0.0).astype(HALF)
        return carry

    lax.fori_loop(0, count // LANES, choose, 0)

    for n, (src, dst) in enumerate(weights):
        weight_crossed[n].wait()
        weight_done.append(push(dst.at[far], dst.at[far], send, recv, 6 + 3 * n, sibling))
    mine[3].wait()
    pair[3].wait()

    arrived = returned.at[core]
    pltpu.make_async_copy(arrived, arrived, part_recv).wait()
    push(arrived, arrived, send, recv, 13, sibling).wait()

    values = returned[...].reshape(2 * halo_rows, LANES)
    sent = []
    for n in range(STEPS):
        rows = pl.ds(n * step_rows, step_rows)
        total = jnp.dot(pick[rows, :], values, preferred_element_type=FLOAT)
        total += own_mine[half, rows, :].astype(FLOAT) + own_in[half, rows, :].astype(FLOAT)
        own_cross[n].wait()
        summed[half, rows, :] = (total + own_far[rows, :].astype(FLOAT)).astype(HALF)
        piece = summed.at[half, rows, :]
        sent.append(push(piece, piece, row_send, row_recv, n, across))

    load.wait()
    for copy in weight_done:
        copy.wait()
    first_layer = all_in[...].reshape(latent, 2 * latent)
    second_layer = all_out[...].reshape(latent, latent)
    column = jnp.concatenate([all_vectors[c].T[:quarter, :] for c in range(chans)], axis=0)
    bias = jnp.concatenate(
        [jnp.broadcast_to(out_bias[:, n : n + LANES], (8, LANES)).T for n in range(0, latent, LANES)], axis=0
    )
    both = (((1,), (1,)), ((), ()))
    final = []
    for n in range(STEPS):
        rows = pl.ds(n * step_rows, step_rows)
        latents = nodes[:, rows]
        pre = jnp.dot(first_layer[:, :latent], latents, preferred_element_type=FLOAT)
        piece = summed.at[other, rows, :]
        describe(piece, piece, row_send, row_recv, n, across).wait_recv()
        total = jnp.concatenate([summed[0, rows, :], summed[1, rows, :]], axis=1)
        pre += lax.dot_general(first_layer[:, latent:], total, both, preferred_element_type=FLOAT)
        hidden = silu_rows(pre + column[:, 0:1]).astype(HALF)
        post = lax.dot_general(
            second_layer, hidden, (((0,), (0,)), ((), ())), preferred_element_type=FLOAT
        ) + bias[:, 0:1]
        centred = post - jnp.mean(post, axis=0, keepdims=True)
        var = jnp.mean(centred * centred, axis=0, keepdims=True)
        norm = centred * lax.rsqrt(var + 1e-05) * column[:, 1:2] + column[:, 2:3]
        new = (latents.astype(FLOAT) + norm).astype(HALF)
        for c in range(chans):
            fresh[c, :, rows] = new[c * quarter : (c + 1) * quarter, :]
        place = pl.ds(pl.multiple_of(core * count + n * step_rows, step_rows), step_rows)
        final.append(fetch(fresh.at[chan, :, rows], result.at[:, place], end_local, n))
        final.append(
            push(fresh.at[chan + 1 - 2 * core, :, rows], result.at[:, place], end_send, end_recv, n, sibling)
        )

    for copy in sent:
        copy.wait_send()
    gone = reduced.at[pl.ds(0, (parts - 1) * slots), :]
    pltpu.make_async_copy(gone, gone, part_send).wait()
    for copy in final:
        copy.wait()


def reverse(sums, own, rows_of, w_in, w_out, in_bias, out_bias, gain, shift, parts, chans):
    latent, node_rows = own.shape
    count = node_rows // 2
    halo_rows = (sums.shape[0] - 2 * node_rows) // 4
    half = lambda *shape: pltpu.VMEM(shape, HALF)
    dma = lambda count: pltpu.SemaphoreType.DMA((count,))
    return pl.pallas_call(
        functools.partial(reverse_kernel, parts=parts, chans=chans),
        in_specs=[ANY, ANY] + [VMEM] * 7,
        out_specs=VMEM,
        out_shape=jax.ShapeDtypeStruct((latent // chans, node_rows), HALF),
        scratch_shapes=[
            half(2, halo_rows, LANES), half(2, count, LANES),
            half(2, halo_rows, LANES), half(2, count, LANES),
            half(halo_rows, LANES), half(count, LANES),
            half(halo_rows, LANES), half(count, LANES),
            half(halo_rows, LANES), half(2, halo_rows, LANES),
            half(count, 2 * halo_rows), half(latent, count), half(2, count, LANES),
            half(chans, latent // chans, count), pltpu.VMEM((8, LANES), FLOAT),
            half(chans, *w_in.shape), half(chans, *w_out.shape), pltpu.VMEM((chans, 8, LANES), FLOAT),
            pltpu.SemaphoreType.DMA,
            pltpu.SemaphoreType.DMA,
            dma(14), dma(14), dma(5), dma(GROUPS), dma(GROUPS), dma(STEPS), dma(STEPS), dma(STEPS), dma(STEPS),
            dma(STEPS), dma(STEPS), dma(STEPS),
        ],
        compiler_params=pltpu.CompilerParams(
            collective_id=1, has_side_effects=True, vmem_limit_bytes=VMEM_LIMIT
        ),
        name="reverse",
    )(sums, own, rows_of, w_in, w_out, in_bias, out_bias, gain, shift)


def body(
    node_latent,
    edge_latent,
    senders,
    receivers,
    edge_count,
    send_list,
    w_edge_in,
    edge_in_bias,
    w_edge_out,
    edge_out_bias,
    edge_gain,
    edge_shift,
    w_node_in,
    node_in_bias,
    w_node_out,
    node_out_bias,
    node_gain,
    node_shift,
):
    node_rows, quarter = node_latent.shape
    parts = lax.axis_size("dom")
    chans = lax.axis_size("chan")
    chan = lax.axis_index("chan")
    slots = send_list.shape[2]
    edge_rows = edge_latent.shape[0]

    own, halo, sender_rows, receiver_rows = forward(
        send_list[0].T, node_latent.T, senders.reshape(-1, LANES), receivers.reshape(-1, LANES), parts, chans
    )
    live = jnp.clip(edge_count - chan * edge_rows, 0, edge_rows)
    edge_new, sums = edge_block(
        sender_rows.reshape(-1), receiver_rows.reshape(-1), live, own, halo, edge_latent, w_edge_in,
        edge_in_bias, w_edge_out, edge_out_bias, edge_gain, edge_shift,
    )

    rows_of = send_list[0].reshape(parts, 2, slots // 2).transpose(1, 0, 2).reshape(1, parts * slots)
    row = lambda vector: vector.reshape(1, -1)
    node_new = reverse(
        sums, own, rows_of, w_node_in.T, w_node_out, row(node_in_bias), row(node_out_bias),
        row(node_gain), row(node_shift), parts, chans,
    )
    return (node_new.T, edge_new)


def solution(mesh):
    placed = (
        P("dom", "chan"),
        P(("dom", "chan"), None),
        P(("dom", "chan")),
        P(("dom", "chan")),
        P("dom"),
        P("dom", None, None),
        P(),
        P(),
        P(),
        P(),
        P(),
        P(),
        P(None, "chan"),
        P("chan"),
        P("chan", None),
        P(),
        P("chan"),
        P("chan"),
    )
    return jax.shard_map(
        body,
        mesh=mesh,
        in_specs=placed,
        out_specs=(P("dom", "chan"), P(("dom", "chan"), None)),
        check_vma=False,
    )
```

```python
import functools

import jax
import jax.numpy as jnp
from jax import lax
from jax.experimental import pallas as pl
from jax.experimental.pallas import tpu as pltpu
from jax.sharding import PartitionSpec as P

LANES = 128
EDGE_TILE = 128
COPIES = 4
GATHER = 16
CHUNK = 512
GROUPS = 4
STEPS = 5
VMEM_LIMIT = 58 * 2**20
MESH = pl.DeviceIdType.MESH
FLOAT = jnp.float32
HALF = jnp.bfloat16
ANY = pl.BlockSpec(memory_space=pl.ANY)
VMEM = pl.BlockSpec(memory_space=pltpu.VMEM)


def silu_rows(values):
    return values * jax.nn.sigmoid(values)


def offset_of(place, parts):
    return 2 * lax.rem(place, parts // 2) + 1 + place // (parts // 2)


def enter(dom, chan, parts, chans):
    barrier = pltpu.get_barrier_semaphore()

    def greet(k, carry):
        offset = offset_of(k, parts)
        pl.semaphore_signal(
            barrier, inc=1,
            device_id=(lax.rem(dom + offset, parts), lax.rem(chan + 2 * (offset % 2), chans)),
            device_id_type=MESH,
        )
        return carry

    lax.fori_loop(0, parts - 1, greet, 0)
    for k in range(1, chans):
        pl.semaphore_signal(barrier, inc=1, device_id=(dom, lax.rem(chan + k, chans)), device_id_type=MESH)
    pl.semaphore_wait(barrier, parts + chans - 2)


def forward_kernel(
    send_rows, live, nodes, senders, receivers,
    own, halo, sender_rows, receiver_rows,
    wide, stage, outgoing, part_send, part_recv, send, recv, local,
    *, parts, chans,
):
    dom = lax.axis_index("dom")
    chan = lax.axis_index("chan")
    quarter, node_rows = nodes.shape
    slots = send_rows.shape[0] // 2
    half = parts // 2
    sibling = (dom, chan + 1 - 2 * lax.rem(chan, 2))
    far = lax.rem(chan + 2, chans)
    across = (dom, far)
    enter(dom, chan, parts, chans)

    def block(index, n):
        rows = pl.ds(pl.multiple_of(index * quarter, quarter), quarter)
        return own.at[rows, n * node_rows // STEPS : (n + 1) * node_rows // STEPS]

    def push(src, dst, index, target):
        copy = pltpu.make_async_remote_copy(
            src_ref=src, dst_ref=dst, send_sem=send.at[index], recv_sem=recv.at[index],
            device_id=target, device_id_type=MESH,
        )
        copy.start()
        return copy

    crossed, done = [], []

    def push_own(n):
        piece = nodes.at[:, n * node_rows // STEPS : (n + 1) * node_rows // STEPS]
        crossed.append(push(piece, block(chan, n), 3 * (GROUPS + n), across))
        done.append(push(piece, block(chan, n), 3 * (GROUPS + n) + 1, sibling))

    rows = pl.ds(pl.multiple_of(chan * quarter, quarter), quarter)
    keep = pltpu.make_async_copy(nodes, own.at[rows, :], local)
    keep.start()
    for n in range(STEPS):
        push_own(n)

    for start in range(0, node_rows, LANES):
        piece = nodes[:, start : start + LANES].astype(FLOAT)
        wide[pl.ds(start, LANES), :] = jnp.concatenate([piece, piece], axis=0).T

    left = lax.broadcasted_iota(jnp.int32, (1, LANES), 1) < quarter

    def fill(k):
        peer = lax.rem(dom + offset_of(k, parts), parts)
        base = pl.multiple_of(k * slots, slots)
        rows = []
        for j in range(slots):
            low = wide[pl.ds(send_rows[j, peer], 1), :]
            high = wide[pl.ds(send_rows[j + slots, peer], 1), :]
            rows.append(jnp.where(left, low, high))
        for j in range(slots):
            stage[pl.ds(base + j, 1), :] = rows[j]
        outgoing[k] = stage[pl.ds(base, slots), :].astype(HALF)
        return peer, base

    group = parts // GROUPS

    def send_part(k, carry):
        peer, base = fill(k)
        target = lax.rem(chan + 2 * (1 - k // half), chans)
        pltpu.make_async_remote_copy(
            src_ref=outgoing.at[k], dst_ref=halo.at[chan, pl.ds(base, slots), :],
            send_sem=part_send, recv_sem=part_recv.at[k // group],
            device_id=(peer, target), device_id_type=MESH,
        ).start()
        return carry

    crossings, pieces = [], []

    def share(g):
        rows = pl.ds(g * group * slots, group * slots)
        here, there = (far, chan) if g * group < half else (chan, far)
        piece = halo.at[here, rows, :]
        pltpu.make_async_copy(piece, piece, part_recv.at[g]).wait()
        crossings.append(push(piece, piece, 3 * g, across))
        done.append(push(piece, piece, 1 + 3 * g, sibling))
        pieces.append(halo.at[there, rows, :])

    for g in range(GROUPS):
        lax.fori_loop(g * group, min((g + 1) * group, parts - 1), send_part, 0)
    _, base = fill(parts - 1)
    mine = pltpu.make_async_copy(
        outgoing.at[parts - 1], halo.at[chan, pl.ds(base, slots), :], part_recv.at[GROUPS - 1]
    )
    mine.start()

    sender_rows[...] = 2 * senders[...]
    index = receivers[...]
    slot = index - node_rows
    offset = (dom + 2 * parts - 1 - (slot >> 5)) & (parts - 1)
    place = (offset >> 1) + half * (offset & 1)
    halo_row = node_rows + ((slot >> 4) & 1) * (parts * slots) + place * slots + (slot & 15)
    index = jnp.where(index < node_rows, index, halo_row)
    edge = LANES * lax.broadcasted_iota(jnp.int32, index.shape, 0) + lax.broadcasted_iota(jnp.int32, index.shape, 1)
    receiver_rows[...] = 2 * jnp.where(edge < live[0], index, node_rows + 2 * parts * slots)

    for g in range(GROUPS):
        share(g)
    for n in range(STEPS):
        crossed[n].wait_recv()
        done.append(push(block(far, n), block(far, n), 3 * (GROUPS + n) + 2, sibling))
    for g, piece in enumerate(pieces):
        pltpu.make_async_remote_copy(
            src_ref=piece, dst_ref=piece, send_sem=send.at[3 * g], recv_sem=recv.at[3 * g],
            device_id=across, device_id_type=MESH,
        ).wait_recv()
        done.append(push(piece, piece, 2 + 3 * g, sibling))
    for copy in done:
        copy.wait()
    for copy in crossed:
        copy.wait_send()
    for copy in crossings:
        copy.wait_send()
    keep.wait()
    sent = outgoing.at[pl.ds(0, parts - 1)]
    pltpu.make_async_copy(sent, sent, part_send).wait()


def forward(send_rows, live, nodes, senders, receivers, parts, chans):
    quarter, node_rows = nodes.shape
    slots = send_rows.shape[0]
    rows = parts * slots // 2
    copies = 3 * (STEPS + GROUPS)
    return pl.pallas_call(
        functools.partial(forward_kernel, parts=parts, chans=chans),
        in_specs=[pl.BlockSpec(memory_space=pltpu.SMEM)] * 2 + [VMEM] * 3,
        out_specs=[ANY] * 2 + [VMEM] * 2,
        out_shape=[
            jax.ShapeDtypeStruct((chans * quarter, node_rows), HALF),
            jax.ShapeDtypeStruct((chans, rows, LANES), HALF),
            jax.ShapeDtypeStruct(senders.shape, senders.dtype),
            jax.ShapeDtypeStruct(receivers.shape, receivers.dtype),
        ],
        scratch_shapes=[
            pltpu.VMEM((node_rows, LANES), FLOAT),
            pltpu.VMEM((rows, LANES), FLOAT),
            pltpu.VMEM((parts, slots // 2, LANES), HALF),
            pltpu.SemaphoreType.DMA,
            pltpu.SemaphoreType.DMA((GROUPS,)),
            pltpu.SemaphoreType.DMA((copies,)),
            pltpu.SemaphoreType.DMA((copies,)),
            pltpu.SemaphoreType.DMA,
        ],
        compiler_params=pltpu.CompilerParams(
            collective_id=0, has_side_effects=True, vmem_limit_bytes=VMEM_LIMIT
        ),
        name="forward",
    )(send_rows, live, nodes, senders, receivers)


def edge_kernel(
    live, senders_in, receivers_in, own_in, halo_in, edges_in, w_in_in, b_in, w_out, b_out, gain, shift,
    edge_new, sums,
    senders, receivers, own, halo, edges, w_in, fresh, totals, sent, received, gathered0, gathered1, messages0, messages1, loads, tile_out, sum_out,
    *partial,
):
    gathered = (gathered0, gathered1)
    messages = (messages0, messages1)
    tile = messages0.shape[0] // 2
    edge_rows, latent = edges.shape
    node_rows = own.shape[1]
    chans, halo_rows, _ = halo.shape
    quarter = latent // chans
    steps = edge_rows // tile

    loading = []
    for n, (src, dst) in enumerate((
        (own_in, own), (w_in_in, w_in), (halo_in, halo), (senders_in, senders), (receivers_in, receivers), (edges_in, edges)
    )):
        loading.append(pltpu.make_async_copy(src, dst, loads.at[n]))
        loading[-1].start()
    for part in partial:
        part[...] = jnp.zeros_like(part)
    loading[0].wait()
    loading[1].wait()
    across = (((0,), (0,)), ((), ()))
    for start in range(0, node_rows, CHUNK):
        block = own[:, start : start + CHUNK]
        for target, first in ((sent, latent), (received, 2 * latent)):
            result = lax.dot_general(
                block, w_in[first : first + latent, :], across, preferred_element_type=FLOAT
            )
            target[pl.ds(2 * start, CHUNK, stride=2), :] = result[:, :LANES]
            target[pl.ds(2 * start + 1, CHUNK, stride=2), :] = result[:, LANES:]
    weights = [w_in[2 * latent + c * quarter : 2 * latent + (c + 1) * quarter, :] for c in range(chans)]
    zero = jnp.zeros_like(weights[0])
    halves = []
    for side in range(2):
        padded = [[w, zero] if side == 0 else [zero, w] for w in weights]
        halves.append([
            jnp.concatenate(padded[c] + padded[c + 1], axis=0) for c in range(0, chans, 2)
        ])
    loading[2].wait()
    for start in range(0, halo_rows, CHUNK):
        blocks = [
            jnp.concatenate([halo[c, start : start + CHUNK, :], halo[c + 1, start : start + CHUNK, :]], axis=1)
            for c in range(0, chans, 2)
        ]
        for side in range(2):
            result = sum(
                jnp.dot(b, w, preferred_element_type=FLOAT) for b, w in zip(blocks, halves[side])
            )
            at = 2 * (node_rows + side * halo_rows + start)
            received[pl.ds(at, CHUNK, stride=2), :] = result[:, :LANES]
            received[pl.ds(at + 1, CHUNK, stride=2), :] = result[:, LANES:]
    for copy in loading[3:]:
        copy.wait()

    def gather(base, target):
        for first in range(0, tile, GATHER):
            rows = []
            for u in range(first, first + GATHER):
                rows.append(sent[pl.ds(senders[base + u], 2), :] + received[pl.ds(receivers[base + u], 2), :])
            for u in range(GATHER):
                target[2 * (first + u) : 2 * (first + u) + 2, :] = rows[u]

    def scatter(base, source):
        for first in range(0, tile, COPIES):
            places = [pl.ds(receivers[base + first + u], 2) for u in range(COPIES)]
            new_rows = [
                partial[u][places[u], :] + source[2 * (first + u) : 2 * (first + u) + 2, :] for u in range(COPIES)
            ]
            for u in range(COPIES):
                partial[u][places[u], :] = new_rows[u]

    def dense(base, source, target):
        latents = edges[pl.ds(base, tile), :]
        pre = jnp.dot(latents, w_in[:latent, :], preferred_element_type=FLOAT)
        low = pre[:, :LANES] + source[pl.ds(0, tile, stride=2), :]
        high = pre[:, LANES:] + source[pl.ds(1, tile, stride=2), :]
        hidden = silu_rows(jnp.concatenate([low, high], axis=1) + b_in[...]).astype(HALF)
        post = jnp.dot(hidden, w_out[...], preferred_element_type=FLOAT) + b_out[...]
        centred = post - jnp.mean(post, axis=-1, keepdims=True)
        var = jnp.mean(centred * centred, axis=-1, keepdims=True)
        norm = centred * lax.rsqrt(var + 1e-05) * gain[...] + shift[...]
        row = lax.broadcasted_iota(jnp.int32, (tile, 1), 0) + base
        norm = jnp.where(row < live[0], norm, 0.0)
        new = (latents.astype(FLOAT) + norm).astype(HALF)
        fresh[pl.ds(base, tile), :] = new
        full = new.astype(FLOAT)
        target[pl.ds(0, tile, stride=2), :] = full[:, :LANES]
        target[pl.ds(1, tile, stride=2), :] = full[:, LANES:]

    def two_tiles(k, carry):
        for p in range(2):
            step = 2 * k + p
            base = pl.multiple_of(step * tile, tile)
            gather(jnp.minimum(step + 1, steps - 1) * tile, gathered[1 - p])
            dense(base, gathered[p], messages[p])
            scatter(jnp.maximum(step - 1, 0) * tile, messages[1 - p])
        rows = pl.ds(pl.multiple_of(2 * k * tile, 2 * tile), 2 * tile)
        pltpu.make_async_copy(fresh.at[rows, :], edge_new.at[rows, :], tile_out).start()
        return carry

    messages1[...] = jnp.zeros_like(messages1)
    gather(0, gathered0)
    lax.fori_loop(0, steps // 2, two_tiles, 0)
    scatter((steps - 1) * tile, messages1)

    table_rows = sums.shape[0] // 2
    pieces = 3
    piece_rows = table_rows // pieces

    def total_chunk(k, carry):
        start = pl.multiple_of(k * CHUNK, CHUNK)
        for lanes in range(2):
            rows = pl.ds(2 * start + lanes, CHUNK, stride=2)
            total = partial[0][rows, :]
            for part in partial[1:]:
                total += part[rows, :]
            totals[pl.ds(lanes * table_rows + start, CHUNK), :] = total.astype(sums.dtype)
        return carry

    leaving = []
    for n in range(pieces):
        chunks = piece_rows // CHUNK
        lax.fori_loop(n * chunks, (n + 1) * chunks, total_chunk, 0)
        for lanes in range(2):
            rows = pl.ds(lanes * table_rows + n * piece_rows, piece_rows)
            leaving.append(pltpu.make_async_copy(totals.at[rows, :], sums.at[rows, :], sum_out.at[2 * n + lanes]))
            leaving[-1].start()
    for copy in leaving:
        copy.wait()
    pltpu.make_async_copy(fresh, edge_new, tile_out).wait()


def edge_block(senders, receivers, live, own, halo, edges, w_in, b_in, w_out, b_out, gain, shift):
    edge_rows, latent = edges.shape
    node_rows = own.shape[1]
    table_rows = node_rows + 2 * halo.shape[1]
    scratch = lambda rows: pltpu.VMEM((2 * rows, LANES), FLOAT)
    like = lambda array: pltpu.VMEM(array.shape, array.dtype)
    b_in, b_out, gain, shift = (v.reshape(1, latent) for v in (b_in, b_out, gain, shift))
    return pl.pallas_call(
        edge_kernel,
        in_specs=[pl.BlockSpec(memory_space=pltpu.SMEM)] + [ANY] * 6 + [VMEM] * 5,
        out_specs=[ANY] * 2,
        scratch_shapes=[
            pltpu.SMEM(senders.shape, senders.dtype), pltpu.SMEM(receivers.shape, receivers.dtype),
            like(own), like(halo), like(edges), like(w_in), like(edges), pltpu.VMEM((2 * table_rows, LANES), HALF),
            scratch(node_rows), scratch(table_rows + 4), *[scratch(EDGE_TILE)] * 4,
            pltpu.SemaphoreType.DMA((6,)), pltpu.SemaphoreType.DMA, pltpu.SemaphoreType.DMA((6,)),
        ] + [scratch(table_rows + 4)] * COPIES,
        out_shape=[
            jax.ShapeDtypeStruct((edge_rows, latent), HALF),
            jax.ShapeDtypeStruct((2 * table_rows, LANES), HALF),
        ],
        compiler_params=pltpu.CompilerParams(vmem_limit_bytes=VMEM_LIMIT),
        name="edges",
    )(live, senders, receivers, own, halo, edges, w_in, b_in, w_out, b_out, gain, shift)


def reverse_kernel(
    sums, own, rows_of, w_in, w_out, in_bias, out_bias, gain, shift,
    result,
    halo_in, own_in, halo_mine, own_mine, halo_out, own_out, halo_far, own_far, reduced, returned,
    pick, nodes, summed, fresh, vectors, all_in, all_out, all_vectors,
    part_send, part_recv, send, recv, local, halo_send, halo_recv, own_send, own_recv, row_send, row_recv,
    end_send, end_recv, end_local,
    *, parts, chans,
):
    dom = lax.axis_index("dom")
    chan = lax.axis_index("chan")
    side = chan // 2
    core = lax.rem(chan, 2)
    half = lax.rem(side + dom, 2)
    other = 1 - half
    far = lax.rem(chan + 2, chans)
    sibling = (dom, chan + 1 - 2 * core)
    across = (dom, far)
    latent, count = nodes.shape
    quarter = latent // chans
    halo_rows = reduced.shape[0]
    slots = halo_rows // parts
    table_rows = sums.shape[0] // 2

    def own_block(lanes, index):
        return sums.at[pl.ds(pl.multiple_of(lanes * table_rows + index * count, LANES), count), :]

    def halo_block(lanes, index):
        start = pl.multiple_of(lanes * table_rows + 2 * count + index * halo_rows, LANES)
        return sums.at[pl.ds(start, halo_rows), :]

    def describe(src, dst, sends, recvs, index, target):
        return pltpu.make_async_remote_copy(
            src_ref=src, dst_ref=dst, send_sem=sends.at[index], recv_sem=recvs.at[index],
            device_id=target, device_id_type=MESH,
        )

    def push(*where):
        copy = describe(*where)
        copy.start()
        return copy

    def fetch(src, dst, sems, index):
        copy = pltpu.make_async_copy(src, dst, sems.at[index])
        copy.start()
        return copy

    columns = pl.ds(pl.multiple_of(core * count, count), count)
    mine = [
        fetch(halo_block(other, core), halo_mine.at[other], local, 0),
        fetch(own_block(other, core), own_mine.at[other], local, 1),
        fetch(halo_block(half, core), halo_mine.at[half], local, 2),
        fetch(own_block(half, core), own_mine.at[half], local, 3),
    ]
    load = fetch(own.at[:, columns], nodes, local, 4)
    vectors[...] = jnp.zeros_like(vectors)
    for n, values in enumerate((in_bias, gain, shift)):
        vectors[n : n + 1, :quarter] = values[...].astype(FLOAT)
    enter(dom, chan, parts, chans)

    pair = [
        push(halo_block(other, 1 - core), halo_in.at[other], send, recv, 0, sibling),
        push(own_block(other, 1 - core), own_in.at[other], send, recv, 1, sibling),
        push(halo_block(half, 1 - core), halo_in.at[half], send, recv, 2, sibling),
        push(own_block(half, 1 - core), own_in.at[half], send, recv, 3, sibling),
    ]
    weights = [(w_in, all_in), (w_out, all_out), (vectors, all_vectors)]
    weight_crossed, weight_done = [], []
    for n, (src, dst) in enumerate(weights):
        weight_crossed.append(push(src, dst.at[chan], send, recv, 4 + 3 * n, across))
        weight_done.append(push(src, dst.at[chan], send, recv, 5 + 3 * n, sibling))
        dst[chan] = src[...]

    group_rows = halo_rows // GROUPS
    step_rows = count // STEPS
    mine[0].wait()
    pair[0].wait()
    halo_cross, own_cross = [], []
    for g in range(GROUPS):
        rows = pl.ds(g * group_rows, group_rows)
        halo_out[rows, :] = (
            halo_mine[other, rows, :].astype(FLOAT) + halo_in[other, rows, :].astype(FLOAT)
        ).astype(HALF)
        halo_cross.append(push(halo_out.at[rows, :], halo_far.at[rows, :], halo_send, halo_recv, g, across))
    mine[1].wait()
    pair[1].wait()
    for n in range(STEPS):
        rows = pl.ds(n * step_rows, step_rows)
        own_out[rows, :] = (
            own_mine[other, rows, :].astype(FLOAT) + own_in[other, rows, :].astype(FLOAT)
        ).astype(HALF)
        own_cross.append(push(own_out.at[rows, :], own_far.at[rows, :], own_send, own_recv, n, across))

    def send_part(k, carry):
        offset = offset_of(k, parts)
        rows = pl.ds(pl.multiple_of(k * slots, slots), slots)
        landing = pl.ds(pl.multiple_of(dom * slots, slots), slots)
        pltpu.make_async_remote_copy(
            src_ref=reduced.at[rows, :], dst_ref=returned.at[core, landing, :],
            send_sem=part_send, recv_sem=part_recv,
            device_id=(lax.rem(dom + parts - offset, parts), lax.rem(chan + 2 * (offset % 2), chans)),
            device_id_type=MESH,
        ).start()
        return carry

    mine[2].wait()
    pair[2].wait()
    group = parts // GROUPS
    for g in range(GROUPS):
        rows = pl.ds(g * group_rows, group_rows)
        halo_cross[g].wait()
        reduced[rows, :] = (
            halo_mine[half, rows, :].astype(FLOAT)
            + halo_in[half, rows, :].astype(FLOAT)
            + halo_far[rows, :].astype(FLOAT)
        ).astype(HALF)
        lax.fori_loop(g * group, min((g + 1) * group, parts - 1), send_part, 0)
    last = pl.ds((parts - 1) * slots, slots)
    landing = pl.ds(pl.multiple_of(dom * slots, slots), slots)
    pltpu.make_async_copy(reduced.at[last, :], returned.at[core, landing, :], part_recv).start()

    def choose(n, carry):
        start = pl.multiple_of(n * LANES, LANES)
        row = lax.broadcasted_iota(jnp.int32, (LANES, 1), 0) + (start + core * count)
        pick[pl.ds(start, LANES), :] = jnp.where(rows_of[...] == row, 1.0, 0.0).astype(HALF)
        return carry

    lax.fori_loop(0, count // LANES, choose, 0)

    for n, (src, dst) in enumerate(weights):
        weight_crossed[n].wait()
        weight_done.append(push(dst.at[far], dst.at[far], send, recv, 6 + 3 * n, sibling))
    mine[3].wait()
    pair[3].wait()

    arrived = returned.at[core]
    pltpu.make_async_copy(arrived, arrived, part_recv).wait()
    push(arrived, arrived, send, recv, 13, sibling).wait()

    values = returned[...].reshape(2 * halo_rows, LANES)
    sent = []
    for n in range(STEPS):
        rows = pl.ds(n * step_rows, step_rows)
        total = jnp.dot(pick[rows, :], values, preferred_element_type=FLOAT)
        total += own_mine[half, rows, :].astype(FLOAT) + own_in[half, rows, :].astype(FLOAT)
        own_cross[n].wait()
        summed[half, rows, :] = (total + own_far[rows, :].astype(FLOAT)).astype(HALF)
        piece = summed.at[half, rows, :]
        sent.append(push(piece, piece, row_send, row_recv, n, across))

    load.wait()
    for copy in weight_done:
        copy.wait()
    first_layer = all_in[...].reshape(latent, 2 * latent)
    second_layer = all_out[...].reshape(latent, latent)
    column = jnp.concatenate([all_vectors[c].T[:quarter, :] for c in range(chans)], axis=0)
    bias = jnp.concatenate(
        [jnp.broadcast_to(out_bias[:, n : n + LANES], (8, LANES)).T for n in range(0, latent, LANES)], axis=0
    )
    both = (((1,), (1,)), ((), ()))
    final = []
    for n in range(STEPS):
        rows = pl.ds(n * step_rows, step_rows)
        latents = nodes[:, rows]
        pre = jnp.dot(first_layer[:, :latent], latents, preferred_element_type=FLOAT)
        piece = summed.at[other, rows, :]
        describe(piece, piece, row_send, row_recv, n, across).wait_recv()
        total = jnp.concatenate([summed[0, rows, :], summed[1, rows, :]], axis=1)
        pre += lax.dot_general(first_layer[:, latent:], total, both, preferred_element_type=FLOAT)
        hidden = silu_rows(pre + column[:, 0:1]).astype(HALF)
        post = lax.dot_general(
            second_layer, hidden, (((0,), (0,)), ((), ())), preferred_element_type=FLOAT
        ) + bias[:, 0:1]
        centred = post - jnp.mean(post, axis=0, keepdims=True)
        var = jnp.mean(centred * centred, axis=0, keepdims=True)
        norm = centred * lax.rsqrt(var + 1e-05) * column[:, 1:2] + column[:, 2:3]
        new = (latents.astype(FLOAT) + norm).astype(HALF)
        for c in range(chans):
            fresh[c, :, rows] = new[c * quarter : (c + 1) * quarter, :]
        place = pl.ds(pl.multiple_of(core * count + n * step_rows, step_rows), step_rows)
        final.append(fetch(fresh.at[chan, :, rows], result.at[:, place], end_local, n))
        final.append(
            push(fresh.at[chan + 1 - 2 * core, :, rows], result.at[:, place], end_send, end_recv, n, sibling)
        )

    for copy in sent:
        copy.wait_send()
    gone = reduced.at[pl.ds(0, (parts - 1) * slots), :]
    pltpu.make_async_copy(gone, gone, part_send).wait()
    for copy in final:
        copy.wait()


def reverse(sums, own, rows_of, w_in, w_out, in_bias, out_bias, gain, shift, parts, chans):
    latent, node_rows = own.shape
    count = node_rows // 2
    halo_rows = (sums.shape[0] - 2 * node_rows) // 4
    half = lambda *shape: pltpu.VMEM(shape, HALF)
    dma = lambda count: pltpu.SemaphoreType.DMA((count,))
    return pl.pallas_call(
        functools.partial(reverse_kernel, parts=parts, chans=chans),
        in_specs=[ANY, ANY] + [VMEM] * 7,
        out_specs=VMEM,
        out_shape=jax.ShapeDtypeStruct((latent // chans, node_rows), HALF),
        scratch_shapes=[
            half(2, halo_rows, LANES), half(2, count, LANES),
            half(2, halo_rows, LANES), half(2, count, LANES),
            half(halo_rows, LANES), half(count, LANES),
            half(halo_rows, LANES), half(count, LANES),
            half(halo_rows, LANES), half(2, halo_rows, LANES),
            half(count, 2 * halo_rows), half(latent, count), half(2, count, LANES),
            half(chans, latent // chans, count), pltpu.VMEM((8, LANES), FLOAT),
            half(chans, *w_in.shape), half(chans, *w_out.shape), pltpu.VMEM((chans, 8, LANES), FLOAT),
            pltpu.SemaphoreType.DMA,
            pltpu.SemaphoreType.DMA,
            dma(14), dma(14), dma(5), dma(GROUPS), dma(GROUPS), dma(STEPS), dma(STEPS), dma(STEPS), dma(STEPS),
            dma(STEPS), dma(STEPS), dma(STEPS),
        ],
        compiler_params=pltpu.CompilerParams(
            collective_id=1, has_side_effects=True, vmem_limit_bytes=53 * 2**20
        ),
        name="reverse",
    )(sums, own, rows_of, w_in, w_out, in_bias, out_bias, gain, shift)


def body(
    node_latent,
    edge_latent,
    senders,
    receivers,
    edge_count,
    send_list,
    w_edge_in,
    edge_in_bias,
    w_edge_out,
    edge_out_bias,
    edge_gain,
    edge_shift,
    w_node_in,
    node_in_bias,
    w_node_out,
    node_out_bias,
    node_gain,
    node_shift,
):
    node_rows, quarter = node_latent.shape
    parts = lax.axis_size("dom")
    chans = lax.axis_size("chan")
    chan = lax.axis_index("chan")
    slots = send_list.shape[2]
    edge_rows = edge_latent.shape[0]

    live = jnp.clip(edge_count - chan * edge_rows, 0, edge_rows)
    own, halo, sender_rows, receiver_rows = forward(
        send_list[0].T, live, node_latent.T, senders.reshape(-1, LANES), receivers.reshape(-1, LANES), parts, chans
    )
    edge_new, sums = edge_block(
        sender_rows.reshape(-1), receiver_rows.reshape(-1), live, own, halo, edge_latent, w_edge_in,
        edge_in_bias, w_edge_out, edge_out_bias, edge_gain, edge_shift,
    )

    rows_of = send_list[0].reshape(parts, 2, slots // 2).transpose(1, 0, 2).reshape(1, parts * slots)
    row = lambda vector: vector.reshape(1, -1)
    node_new = reverse(
        sums, own, rows_of, w_node_in.T, w_node_out, row(node_in_bias), row(node_out_bias),
        row(node_gain), row(node_shift), parts, chans,
    )
    return (node_new.T, edge_new)


def solution(mesh):
    placed = (
        P("dom", "chan"),
        P(("dom", "chan"), None),
        P(("dom", "chan")),
        P(("dom", "chan")),
        P("dom"),
        P("dom", None, None),
        P(),
        P(),
        P(),
        P(),
        P(),
        P(),
        P(None, "chan"),
        P("chan"),
        P("chan", None),
        P(),
        P("chan"),
        P("chan"),
    )
    return jax.shard_map(
        body,
        mesh=mesh,
        in_specs=placed,
        out_specs=(P("dom", "chan"), P(("dom", "chan"), None)),
        check_vma=False,
    )
```

```python
import functools

import jax
import jax.numpy as jnp
from jax import lax
from jax.experimental import pallas as pl
from jax.experimental.pallas import tpu as pltpu
from jax.sharding import PartitionSpec as P

LANES = 128
EDGE_TILE = 192
COPIES = 6
GATHER = 16
CHUNK = 512
GROUPS = 4
STEPS = 5
VMEM_LIMIT = 58 * 2**20
MESH = pl.DeviceIdType.MESH
FLOAT = jnp.float32
HALF = jnp.bfloat16
ANY = pl.BlockSpec(memory_space=pl.ANY)
VMEM = pl.BlockSpec(memory_space=pltpu.VMEM)


def silu_rows(values):
    return values * jax.nn.sigmoid(values)


def offset_of(place, parts):
    return 2 * lax.rem(place, parts // 2) + 1 + place // (parts // 2)


def enter(dom, chan, parts, chans):
    barrier = pltpu.get_barrier_semaphore()

    def greet(k, carry):
        offset = offset_of(k, parts)
        pl.semaphore_signal(
            barrier, inc=1,
            device_id=(lax.rem(dom + offset, parts), lax.rem(chan + 2 * (offset % 2), chans)),
            device_id_type=MESH,
        )
        return carry

    lax.fori_loop(0, parts - 1, greet, 0)
    for k in range(1, chans):
        pl.semaphore_signal(barrier, inc=1, device_id=(dom, lax.rem(chan + k, chans)), device_id_type=MESH)
    pl.semaphore_wait(barrier, parts + chans - 2)


def forward_kernel(
    send_rows, live, nodes, senders, receivers,
    own, halo, sender_rows, receiver_rows,
    wide, stage, outgoing, part_send, part_recv, send, recv, local,
    *, parts, chans,
):
    dom = lax.axis_index("dom")
    chan = lax.axis_index("chan")
    quarter, node_rows = nodes.shape
    slots = send_rows.shape[0] // 2
    half = parts // 2
    sibling = (dom, chan + 1 - 2 * lax.rem(chan, 2))
    far = lax.rem(chan + 2, chans)
    across = (dom, far)
    enter(dom, chan, parts, chans)

    def block(index, n):
        rows = pl.ds(pl.multiple_of(index * quarter, quarter), quarter)
        return own.at[rows, n * node_rows // STEPS : (n + 1) * node_rows // STEPS]

    def push(src, dst, index, target):
        copy = pltpu.make_async_remote_copy(
            src_ref=src, dst_ref=dst, send_sem=send.at[index], recv_sem=recv.at[index],
            device_id=target, device_id_type=MESH,
        )
        copy.start()
        return copy

    crossed, done = [], []

    def push_own(n):
        piece = nodes.at[:, n * node_rows // STEPS : (n + 1) * node_rows // STEPS]
        crossed.append(push(piece, block(chan, n), 3 * (GROUPS + n), across))
        done.append(push(piece, block(chan, n), 3 * (GROUPS + n) + 1, sibling))

    rows = pl.ds(pl.multiple_of(chan * quarter, quarter), quarter)
    keep = pltpu.make_async_copy(nodes, own.at[rows, :], local)
    keep.start()
    for n in range(STEPS):
        push_own(n)

    for start in range(0, node_rows, LANES):
        piece = nodes[:, start : start + LANES].astype(FLOAT)
        wide[pl.ds(start, LANES), :] = jnp.concatenate([piece, piece], axis=0).T

    left = lax.broadcasted_iota(jnp.int32, (1, LANES), 1) < quarter

    def fill(k):
        peer = lax.rem(dom + offset_of(k, parts), parts)
        base = pl.multiple_of(k * slots, slots)
        rows = []
        for j in range(slots):
            low = wide[pl.ds(send_rows[j, peer], 1), :]
            high = wide[pl.ds(send_rows[j + slots, peer], 1), :]
            rows.append(jnp.where(left, low, high))
        for j in range(slots):
            stage[pl.ds(base + j, 1), :] = rows[j]
        outgoing[k] = stage[pl.ds(base, slots), :].astype(HALF)
        return peer, base

    group = parts // GROUPS

    def send_part(k, carry):
        peer, base = fill(k)
        target = lax.rem(chan + 2 * (1 - k // half), chans)
        pltpu.make_async_remote_copy(
            src_ref=outgoing.at[k], dst_ref=halo.at[chan, pl.ds(base, slots), :],
            send_sem=part_send, recv_sem=part_recv.at[k // group],
            device_id=(peer, target), device_id_type=MESH,
        ).start()
        return carry

    crossings, pieces = [], []

    def share(g):
        rows = pl.ds(g * group * slots, group * slots)
        here, there = (far, chan) if g * group < half else (chan, far)
        piece = halo.at[here, rows, :]
        pltpu.make_async_copy(piece, piece, part_recv.at[g]).wait()
        crossings.append(push(piece, piece, 3 * g, across))
        done.append(push(piece, piece, 1 + 3 * g, sibling))
        pieces.append(halo.at[there, rows, :])

    for g in range(GROUPS):
        lax.fori_loop(g * group, min((g + 1) * group, parts - 1), send_part, 0)
    _, base = fill(parts - 1)
    mine = pltpu.make_async_copy(
        outgoing.at[parts - 1], halo.at[chan, pl.ds(base, slots), :], part_recv.at[GROUPS - 1]
    )
    mine.start()

    sender_rows[...] = 2 * senders[...]
    index = receivers[...]
    slot = index - node_rows
    offset = (dom + 2 * parts - 1 - (slot >> 5)) & (parts - 1)
    place = (offset >> 1) + half * (offset & 1)
    halo_row = node_rows + ((slot >> 4) & 1) * (parts * slots) + place * slots + (slot & 15)
    index = jnp.where(index < node_rows, index, halo_row)
    edge = LANES * lax.broadcasted_iota(jnp.int32, index.shape, 0) + lax.broadcasted_iota(jnp.int32, index.shape, 1)
    left_over = live[0] - chan * senders.shape[0] * LANES
    receiver_rows[...] = 2 * jnp.where(edge < left_over, index, node_rows + 2 * parts * slots)

    for g in range(GROUPS):
        share(g)
    for n in range(STEPS):
        crossed[n].wait_recv()
        done.append(push(block(far, n), block(far, n), 3 * (GROUPS + n) + 2, sibling))
    for g, piece in enumerate(pieces):
        pltpu.make_async_remote_copy(
            src_ref=piece, dst_ref=piece, send_sem=send.at[3 * g], recv_sem=recv.at[3 * g],
            device_id=across, device_id_type=MESH,
        ).wait_recv()
        done.append(push(piece, piece, 2 + 3 * g, sibling))
    for copy in done:
        copy.wait()
    for copy in crossed:
        copy.wait_send()
    for copy in crossings:
        copy.wait_send()
    keep.wait()
    sent = outgoing.at[pl.ds(0, parts - 1)]
    pltpu.make_async_copy(sent, sent, part_send).wait()


def forward(send_rows, live, nodes, senders, receivers, parts, chans):
    quarter, node_rows = nodes.shape
    slots = send_rows.shape[0]
    rows = parts * slots // 2
    copies = 3 * (STEPS + GROUPS)
    return pl.pallas_call(
        functools.partial(forward_kernel, parts=parts, chans=chans),
        in_specs=[pl.BlockSpec(memory_space=pltpu.SMEM)] * 2 + [VMEM] * 3,
        out_specs=[ANY] * 2 + [VMEM] * 2,
        out_shape=[
            jax.ShapeDtypeStruct((chans * quarter, node_rows), HALF),
            jax.ShapeDtypeStruct((chans, rows, LANES), HALF),
            jax.ShapeDtypeStruct(senders.shape, senders.dtype),
            jax.ShapeDtypeStruct(receivers.shape, receivers.dtype),
        ],
        scratch_shapes=[
            pltpu.VMEM((node_rows, LANES), FLOAT),
            pltpu.VMEM((rows, LANES), FLOAT),
            pltpu.VMEM((parts, slots // 2, LANES), HALF),
            pltpu.SemaphoreType.DMA,
            pltpu.SemaphoreType.DMA((GROUPS,)),
            pltpu.SemaphoreType.DMA((copies,)),
            pltpu.SemaphoreType.DMA((copies,)),
            pltpu.SemaphoreType.DMA,
        ],
        compiler_params=pltpu.CompilerParams(
            collective_id=0, has_side_effects=True, vmem_limit_bytes=VMEM_LIMIT
        ),
        name="forward",
    )(send_rows, live, nodes, senders, receivers)


def edge_kernel(
    live, senders_in, receivers_in, own_in, halo_in, edges_in, w_in_in, b_in, w_out, b_out, gain, shift,
    edge_new, sums,
    senders, receivers, own, halo, edges, w_in, fresh, totals, sent, received, gathered0, gathered1, messages0, messages1, loads, tile_out, sum_out,
    *partial,
):
    gathered = (gathered0, gathered1)
    messages = (messages0, messages1)
    tile = messages0.shape[0] // 2
    edge_rows, latent = edges.shape
    node_rows = own.shape[1]
    chans, halo_rows, _ = halo.shape
    quarter = latent // chans
    steps = edge_rows // tile
    count = live[0] - lax.axis_index("chan") * edge_rows

    loading = []
    for n, (src, dst) in enumerate((
        (own_in, own), (w_in_in, w_in), (halo_in, halo), (senders_in, senders), (receivers_in, receivers), (edges_in, edges)
    )):
        loading.append(pltpu.make_async_copy(src, dst, loads.at[n]))
        loading[-1].start()
    for part in partial:
        part[...] = jnp.zeros_like(part)
    loading[0].wait()
    loading[1].wait()
    across = (((0,), (0,)), ((), ()))
    for start in range(0, node_rows, CHUNK):
        block = own[:, start : start + CHUNK]
        for target, first in ((sent, latent), (received, 2 * latent)):
            result = lax.dot_general(
                block, w_in[first : first + latent, :], across, preferred_element_type=FLOAT
            )
            target[pl.ds(2 * start, CHUNK, stride=2), :] = result[:, :LANES]
            target[pl.ds(2 * start + 1, CHUNK, stride=2), :] = result[:, LANES:]
    weights = [w_in[2 * latent + c * quarter : 2 * latent + (c + 1) * quarter, :] for c in range(chans)]
    zero = jnp.zeros_like(weights[0])
    halves = []
    for side in range(2):
        padded = [[w, zero] if side == 0 else [zero, w] for w in weights]
        halves.append([
            jnp.concatenate(padded[c] + padded[c + 1], axis=0) for c in range(0, chans, 2)
        ])
    loading[2].wait()
    for start in range(0, halo_rows, CHUNK):
        blocks = [
            jnp.concatenate([halo[c, start : start + CHUNK, :], halo[c + 1, start : start + CHUNK, :]], axis=1)
            for c in range(0, chans, 2)
        ]
        for side in range(2):
            result = sum(
                jnp.dot(b, w, preferred_element_type=FLOAT) for b, w in zip(blocks, halves[side])
            )
            at = 2 * (node_rows + side * halo_rows + start)
            received[pl.ds(at, CHUNK, stride=2), :] = result[:, :LANES]
            received[pl.ds(at + 1, CHUNK, stride=2), :] = result[:, LANES:]
    for copy in loading[3:]:
        copy.wait()

    def gather(base, target):
        for first in range(0, tile, GATHER):
            rows = []
            for u in range(first, first + GATHER):
                rows.append(sent[pl.ds(senders[base + u], 2), :] + received[pl.ds(receivers[base + u], 2), :])
            for u in range(GATHER):
                target[2 * (first + u) : 2 * (first + u) + 2, :] = rows[u]

    def scatter(base, source):
        for first in range(0, tile, COPIES):
            places = [pl.ds(receivers[base + first + u], 2) for u in range(COPIES)]
            new_rows = [
                partial[u][places[u], :] + source[2 * (first + u) : 2 * (first + u) + 2, :] for u in range(COPIES)
            ]
            for u in range(COPIES):
                partial[u][places[u], :] = new_rows[u]

    def dense(base, source, target):
        latents = edges[pl.ds(base, tile), :]
        pre = jnp.dot(latents, w_in[:latent, :], preferred_element_type=FLOAT)
        low = pre[:, :LANES] + source[pl.ds(0, tile, stride=2), :]
        high = pre[:, LANES:] + source[pl.ds(1, tile, stride=2), :]
        hidden = silu_rows(jnp.concatenate([low, high], axis=1) + b_in[...]).astype(HALF)
        post = jnp.dot(hidden, w_out[...], preferred_element_type=FLOAT) + b_out[...]
        centred = post - jnp.mean(post, axis=-1, keepdims=True)
        var = jnp.mean(centred * centred, axis=-1, keepdims=True)
        norm = centred * lax.rsqrt(var + 1e-05) * gain[...] + shift[...]
        row = lax.broadcasted_iota(jnp.int32, (tile, 1), 0) + base
        norm = jnp.where(row < count, norm, 0.0)
        new = (latents.astype(FLOAT) + norm).astype(HALF)
        fresh[pl.ds(base, tile), :] = new
        full = new.astype(FLOAT)
        target[pl.ds(0, tile, stride=2), :] = full[:, :LANES]
        target[pl.ds(1, tile, stride=2), :] = full[:, LANES:]

    def two_tiles(k, carry):
        for p in range(2):
            step = 2 * k + p
            base = pl.multiple_of(step * tile, tile)
            gather(jnp.minimum(step + 1, steps - 1) * tile, gathered[1 - p])
            dense(base, gathered[p], messages[p])
            scatter(jnp.maximum(step - 1, 0) * tile, messages[1 - p])
        rows = pl.ds(pl.multiple_of(2 * k * tile, 2 * tile), 2 * tile)
        pltpu.make_async_copy(fresh.at[rows, :], edge_new.at[rows, :], tile_out).start()
        return carry

    messages1[...] = jnp.zeros_like(messages1)
    gather(0, gathered0)
    lax.fori_loop(0, steps // 2, two_tiles, 0)
    scatter((steps - 1) * tile, messages1)

    table_rows = sums.shape[0] // 2
    pieces = 3
    piece_rows = table_rows // pieces

    def total_chunk(k, carry):
        start = pl.multiple_of(k * CHUNK, CHUNK)
        for lanes in range(2):
            rows = pl.ds(2 * start + lanes, CHUNK, stride=2)
            total = partial[0][rows, :]
            for part in partial[1:]:
                total += part[rows, :]
            totals[pl.ds(lanes * table_rows + start, CHUNK), :] = total.astype(sums.dtype)
        return carry

    leaving = []
    for n in range(pieces):
        chunks = piece_rows // CHUNK
        lax.fori_loop(n * chunks, (n + 1) * chunks, total_chunk, 0)
        for lanes in range(2):
            rows = pl.ds(lanes * table_rows + n * piece_rows, piece_rows)
            leaving.append(pltpu.make_async_copy(totals.at[rows, :], sums.at[rows, :], sum_out.at[2 * n + lanes]))
            leaving[-1].start()
    for copy in leaving:
        copy.wait()
    pltpu.make_async_copy(fresh, edge_new, tile_out).wait()


def edge_block(senders, receivers, live, own, halo, edges, w_in, b_in, w_out, b_out, gain, shift):
    edge_rows, latent = edges.shape
    node_rows = own.shape[1]
    table_rows = node_rows + 2 * halo.shape[1]
    scratch = lambda rows: pltpu.VMEM((2 * rows, LANES), FLOAT)
    like = lambda array: pltpu.VMEM(array.shape, array.dtype)
    b_in, b_out, gain, shift = (v.reshape(1, latent) for v in (b_in, b_out, gain, shift))
    return pl.pallas_call(
        edge_kernel,
        in_specs=[pl.BlockSpec(memory_space=pltpu.SMEM)] + [ANY] * 6 + [VMEM] * 5,
        out_specs=[ANY] * 2,
        scratch_shapes=[
            pltpu.SMEM(senders.shape, senders.dtype), pltpu.SMEM(receivers.shape, receivers.dtype),
            like(own), like(halo), like(edges), like(w_in), like(edges), pltpu.VMEM((2 * table_rows, LANES), HALF),
            scratch(node_rows), scratch(table_rows + 4), *[scratch(EDGE_TILE)] * 4,
            pltpu.SemaphoreType.DMA((6,)), pltpu.SemaphoreType.DMA, pltpu.SemaphoreType.DMA((6,)),
        ] + [scratch(table_rows + 4)] * COPIES,
        out_shape=[
            jax.ShapeDtypeStruct((edge_rows, latent), HALF),
            jax.ShapeDtypeStruct((2 * table_rows, LANES), HALF),
        ],
        compiler_params=pltpu.CompilerParams(vmem_limit_bytes=VMEM_LIMIT),
        name="edges",
    )(live, senders, receivers, own, halo, edges, w_in, b_in, w_out, b_out, gain, shift)


def reverse_kernel(
    sums, own, rows_of, w_in, w_out, in_bias, out_bias, gain, shift,
    result,
    halo_in, own_in, halo_mine, own_mine, halo_out, own_out, halo_far, own_far, reduced, returned,
    pick, nodes, summed, fresh, vectors, all_in, all_out, all_vectors,
    part_send, part_recv, send, recv, local, halo_send, halo_recv, own_send, own_recv, row_send, row_recv,
    end_send, end_recv, end_local,
    *, parts, chans,
):
    dom = lax.axis_index("dom")
    chan = lax.axis_index("chan")
    side = chan // 2
    core = lax.rem(chan, 2)
    half = lax.rem(side + dom, 2)
    other = 1 - half
    far = lax.rem(chan + 2, chans)
    sibling = (dom, chan + 1 - 2 * core)
    across = (dom, far)
    latent, count = nodes.shape
    quarter = latent // chans
    halo_rows = reduced.shape[0]
    slots = halo_rows // parts
    table_rows = sums.shape[0] // 2

    def own_block(lanes, index):
        return sums.at[pl.ds(pl.multiple_of(lanes * table_rows + index * count, LANES), count), :]

    def halo_block(lanes, index):
        start = pl.multiple_of(lanes * table_rows + 2 * count + index * halo_rows, LANES)
        return sums.at[pl.ds(start, halo_rows), :]

    def describe(src, dst, sends, recvs, index, target):
        return pltpu.make_async_remote_copy(
            src_ref=src, dst_ref=dst, send_sem=sends.at[index], recv_sem=recvs.at[index],
            device_id=target, device_id_type=MESH,
        )

    def push(*where):
        copy = describe(*where)
        copy.start()
        return copy

    def fetch(src, dst, sems, index):
        copy = pltpu.make_async_copy(src, dst, sems.at[index])
        copy.start()
        return copy

    columns = pl.ds(pl.multiple_of(core * count, count), count)
    mine = [
        fetch(halo_block(other, core), halo_mine.at[other], local, 0),
        fetch(own_block(other, core), own_mine.at[other], local, 1),
        fetch(halo_block(half, core), halo_mine.at[half], local, 2),
        fetch(own_block(half, core), own_mine.at[half], local, 3),
    ]
    load = fetch(own.at[:, columns], nodes, local, 4)
    vectors[...] = jnp.zeros_like(vectors)
    for n, values in enumerate((in_bias, gain, shift)):
        vectors[n : n + 1, :quarter] = values[...].astype(FLOAT)
    enter(dom, chan, parts, chans)

    pair = [
        push(halo_block(other, 1 - core), halo_in.at[other], send, recv, 0, sibling),
        push(own_block(other, 1 - core), own_in.at[other], send, recv, 1, sibling),
        push(halo_block(half, 1 - core), halo_in.at[half], send, recv, 2, sibling),
        push(own_block(half, 1 - core), own_in.at[half], send, recv, 3, sibling),
    ]
    weights = [(w_in, all_in), (w_out, all_out), (vectors, all_vectors)]
    weight_crossed, weight_done = [], []
    for n, (src, dst) in enumerate(weights):
        weight_crossed.append(push(src, dst.at[chan], send, recv, 4 + 3 * n, across))
        weight_done.append(push(src, dst.at[chan], send, recv, 5 + 3 * n, sibling))
        dst[chan] = src[...]

    group_rows = halo_rows // GROUPS
    step_rows = count // STEPS
    mine[0].wait()
    pair[0].wait()
    halo_cross, own_cross = [], []
    for g in range(GROUPS):
        rows = pl.ds(g * group_rows, group_rows)
        halo_out[rows, :] = (
            halo_mine[other, rows, :].astype(FLOAT) + halo_in[other, rows, :].astype(FLOAT)
        ).astype(HALF)
        halo_cross.append(push(halo_out.at[rows, :], halo_far.at[rows, :], halo_send, halo_recv, g, across))
    mine[1].wait()
    pair[1].wait()
    for n in range(STEPS):
        rows = pl.ds(n * step_rows, step_rows)
        own_out[rows, :] = (
            own_mine[other, rows, :].astype(FLOAT) + own_in[other, rows, :].astype(FLOAT)
        ).astype(HALF)
        own_cross.append(push(own_out.at[rows, :], own_far.at[rows, :], own_send, own_recv, n, across))

    def send_part(k, carry):
        offset = offset_of(k, parts)
        rows = pl.ds(pl.multiple_of(k * slots, slots), slots)
        landing = pl.ds(pl.multiple_of(dom * slots, slots), slots)
        pltpu.make_async_remote_copy(
            src_ref=reduced.at[rows, :], dst_ref=returned.at[core, landing, :],
            send_sem=part_send, recv_sem=part_recv,
            device_id=(lax.rem(dom + parts - offset, parts), lax.rem(chan + 2 * (offset % 2), chans)),
            device_id_type=MESH,
        ).start()
        return carry

    mine[2].wait()
    pair[2].wait()
    group = parts // GROUPS
    for g in range(GROUPS):
        rows = pl.ds(g * group_rows, group_rows)
        halo_cross[g].wait()
        reduced[rows, :] = (
            halo_mine[half, rows, :].astype(FLOAT)
            + halo_in[half, rows, :].astype(FLOAT)
            + halo_far[rows, :].astype(FLOAT)
        ).astype(HALF)
        lax.fori_loop(g * group, min((g + 1) * group, parts - 1), send_part, 0)
    last = pl.ds((parts - 1) * slots, slots)
    landing = pl.ds(pl.multiple_of(dom * slots, slots), slots)
    pltpu.make_async_copy(reduced.at[last, :], returned.at[core, landing, :], part_recv).start()

    def choose(n, carry):
        start = pl.multiple_of(n * LANES, LANES)
        row = lax.broadcasted_iota(jnp.int32, (LANES, 1), 0) + (start + core * count)
        pick[pl.ds(start, LANES), :] = jnp.where(rows_of[...] == row, 1.0, 0.0).astype(HALF)
        return carry

    lax.fori_loop(0, count // LANES, choose, 0)

    for n, (src, dst) in enumerate(weights):
        weight_crossed[n].wait()
        weight_done.append(push(dst.at[far], dst.at[far], send, recv, 6 + 3 * n, sibling))
    mine[3].wait()
    pair[3].wait()

    arrived = returned.at[core]
    pltpu.make_async_copy(arrived, arrived, part_recv).wait()
    push(arrived, arrived, send, recv, 13, sibling).wait()

    values = returned[...].reshape(2 * halo_rows, LANES)
    sent = []
    for n in range(STEPS):
        rows = pl.ds(n * step_rows, step_rows)
        total = jnp.dot(pick[rows, :], values, preferred_element_type=FLOAT)
        total += own_mine[half, rows, :].astype(FLOAT) + own_in[half, rows, :].astype(FLOAT)
        own_cross[n].wait()
        summed[half, rows, :] = (total + own_far[rows, :].astype(FLOAT)).astype(HALF)
        piece = summed.at[half, rows, :]
        sent.append(push(piece, piece, row_send, row_recv, n, across))

    load.wait()
    for copy in weight_done:
        copy.wait()
    first_layer = all_in[...].reshape(latent, 2 * latent)
    second_layer = all_out[...].reshape(latent, latent)
    column = jnp.concatenate([all_vectors[c].T[:quarter, :] for c in range(chans)], axis=0)
    bias = jnp.concatenate(
        [jnp.broadcast_to(out_bias[:, n : n + LANES], (8, LANES)).T for n in range(0, latent, LANES)], axis=0
    )
    both = (((1,), (1,)), ((), ()))
    final = []
    for n in range(STEPS):
        rows = pl.ds(n * step_rows, step_rows)
        latents = nodes[:, rows]
        pre = jnp.dot(first_layer[:, :latent], latents, preferred_element_type=FLOAT)
        piece = summed.at[other, rows, :]
        describe(piece, piece, row_send, row_recv, n, across).wait_recv()
        total = jnp.concatenate([summed[0, rows, :], summed[1, rows, :]], axis=1)
        pre += lax.dot_general(first_layer[:, latent:], total, both, preferred_element_type=FLOAT)
        hidden = silu_rows(pre + column[:, 0:1]).astype(HALF)
        post = lax.dot_general(
            second_layer, hidden, (((0,), (0,)), ((), ())), preferred_element_type=FLOAT
        ) + bias[:, 0:1]
        centred = post - jnp.mean(post, axis=0, keepdims=True)
        var = jnp.mean(centred * centred, axis=0, keepdims=True)
        norm = centred * lax.rsqrt(var + 1e-05) * column[:, 1:2] + column[:, 2:3]
        new = (latents.astype(FLOAT) + norm).astype(HALF)
        for c in range(chans):
            fresh[c, :, rows] = new[c * quarter : (c + 1) * quarter, :]
        place = pl.ds(pl.multiple_of(core * count + n * step_rows, step_rows), step_rows)
        final.append(fetch(fresh.at[chan, :, rows], result.at[:, place], end_local, n))
        final.append(
            push(fresh.at[chan + 1 - 2 * core, :, rows], result.at[:, place], end_send, end_recv, n, sibling)
        )

    for copy in sent:
        copy.wait_send()
    gone = reduced.at[pl.ds(0, (parts - 1) * slots), :]
    pltpu.make_async_copy(gone, gone, part_send).wait()
    for copy in final:
        copy.wait()


def reverse(sums, own, rows_of, w_in, w_out, in_bias, out_bias, gain, shift, parts, chans):
    latent, node_rows = own.shape
    count = node_rows // 2
    halo_rows = (sums.shape[0] - 2 * node_rows) // 4
    half = lambda *shape: pltpu.VMEM(shape, HALF)
    dma = lambda count: pltpu.SemaphoreType.DMA((count,))
    return pl.pallas_call(
        functools.partial(reverse_kernel, parts=parts, chans=chans),
        in_specs=[ANY, ANY] + [VMEM] * 7,
        out_specs=VMEM,
        out_shape=jax.ShapeDtypeStruct((latent // chans, node_rows), HALF),
        scratch_shapes=[
            half(2, halo_rows, LANES), half(2, count, LANES),
            half(2, halo_rows, LANES), half(2, count, LANES),
            half(halo_rows, LANES), half(count, LANES),
            half(halo_rows, LANES), half(count, LANES),
            half(halo_rows, LANES), half(2, halo_rows, LANES),
            half(count, 2 * halo_rows), half(latent, count), half(2, count, LANES),
            half(chans, latent // chans, count), pltpu.VMEM((8, LANES), FLOAT),
            half(chans, *w_in.shape), half(chans, *w_out.shape), pltpu.VMEM((chans, 8, LANES), FLOAT),
            pltpu.SemaphoreType.DMA,
            pltpu.SemaphoreType.DMA,
            dma(14), dma(14), dma(5), dma(GROUPS), dma(GROUPS), dma(STEPS), dma(STEPS), dma(STEPS), dma(STEPS),
            dma(STEPS), dma(STEPS), dma(STEPS),
        ],
        compiler_params=pltpu.CompilerParams(
            collective_id=1, has_side_effects=True, vmem_limit_bytes=53 * 2**20
        ),
        name="reverse",
    )(sums, own, rows_of, w_in, w_out, in_bias, out_bias, gain, shift)


def body(
    node_latent,
    edge_latent,
    senders,
    receivers,
    edge_count,
    send_list,
    w_edge_in,
    edge_in_bias,
    w_edge_out,
    edge_out_bias,
    edge_gain,
    edge_shift,
    w_node_in,
    node_in_bias,
    w_node_out,
    node_out_bias,
    node_gain,
    node_shift,
):
    node_rows, quarter = node_latent.shape
    parts = lax.axis_size("dom")
    chans = lax.axis_size("chan")
    slots = send_list.shape[2]

    own, halo, sender_rows, receiver_rows = forward(
        send_list[0].T, edge_count, node_latent.T, senders.reshape(-1, LANES), receivers.reshape(-1, LANES), parts, chans
    )
    edge_new, sums = edge_block(
        sender_rows.reshape(-1), receiver_rows.reshape(-1), edge_count, own, halo, edge_latent, w_edge_in,
        edge_in_bias, w_edge_out, edge_out_bias, edge_gain, edge_shift,
    )

    rows_of = send_list[0].reshape(parts, 2, slots // 2).transpose(1, 0, 2).reshape(1, parts * slots)
    row = lambda vector: vector.reshape(1, -1)
    node_new = reverse(
        sums, own, rows_of, w_node_in.T, w_node_out, row(node_in_bias), row(node_out_bias),
        row(node_gain), row(node_shift), parts, chans,
    )
    return (node_new.T, edge_new)


def solution(mesh):
    placed = (
        P("dom", "chan"),
        P(("dom", "chan"), None),
        P(("dom", "chan")),
        P(("dom", "chan")),
        P("dom"),
        P("dom", None, None),
        P(),
        P(),
        P(),
        P(),
        P(),
        P(),
        P(None, "chan"),
        P("chan"),
        P("chan", None),
        P(),
        P("chan"),
        P("chan"),
    )
    return jax.shard_map(
        body,
        mesh=mesh,
        in_specs=placed,
        out_specs=(P("dom", "chan"), P(("dom", "chan"), None)),
        check_vma=False,
    )
```
